32 devices in a mesh: dp: 8 (over z, y), tp: 4 (over x, core).
Axes of the slice: x: 2, y: 2, z: 4, core: 2. Of those that a mesh axis runs over, the one named last changes fastest.
Arguments:
- tokens: bfloat16 [16, 1024, 768], P('dp', 'tp'), may hold values from -6 to 6
- cotangent: bfloat16 [16, 1024, 768], P('dp', 'tp'), may hold values from -6 to 6
- segment_ids: int32 [16, 1024], P('dp', 'tp'), may hold values from 0 to 2, as said below
- valid_mask: int32 [16, 1024], P('dp', 'tp'), may hold values from 0 to 1, as said below
- row_half: int32 [16], P('dp'), may hold values from 0 to 1, as said below
- norm1_gain: float32 [768], replicated, may hold values from 0.5 to 1.5
- norm1_shift: float32 [768], replicated, may hold values from -1 to 1
- qkv_weight: bfloat16 [768, 3, 768], P(None, None, 'tp'), may hold values from -0.21875 to 0.21875
- qkv_bias: float32 [3, 768], P(None, 'tp'), may hold values from -1 to 1
- out_weight: bfloat16 [768, 768], P('tp'), may hold values from -2.5 to 2.5
- out_bias: float32 [768], replicated, may hold values from -1 to 1
- norm2_gain: float32 [768], replicated, may hold values from 0.5 to 1.5
- norm2_shift: float32 [768], replicated, may hold values from -1 to 1
- fc_weight: bfloat16 [768, 3072], P(None, 'tp'), may hold values from -0.21875 to 0.21875
- fc_bias: float32 [3072], P('tp'), may hold values from -1 to 1
- proj_weight: bfloat16 [3072, 768], P('tp'), may hold values from -0.109375 to 0.109375
- proj_bias: float32 [768], replicated, may hold values from -1 to 1
Outputs:
- output: bfloat16 [16, 1024, 768], P('dp', 'tp')
- tokens_grad: float32 [16, 1024, 768], P('dp', 'tp')
- norm1_gain_grad: float32 [768], replicated
- norm1_shift_grad: float32 [768], replicated
- qkv_weight_grad: float32 [768, 3, 768], P(None, None, 'tp')
- qkv_bias_grad: float32 [3, 768], P(None, 'tp')
- out_weight_grad: float32 [768, 768], P('tp')
- out_bias_grad: float32 [768], replicated
- norm2_gain_grad: float32 [768], replicated
- norm2_shift_grad: float32 [768], replicated
- fc_weight_grad: float32 [768, 3072], P(None, 'tp')
- fc_bias_grad: float32 [3072], P('tp')
- proj_weight_grad: float32 [3072, 768], P('tp')
- proj_bias_grad: float32 [768], replicated
The draws below stay inside these ranges and needn't reach their ends.
Inputs may be any that keep to these rules, and one draw needn't show every extreme that they name: `segment_ids`: each row holds three documents numbered 0, 1, 2 in order; document 1 starts at position 128 or earlier, and document 2 starts at position 896 or later and before 1024. `valid_mask`: in each row the tokens with 1 form a prefix of 256 tokens or more. `row_half`: rows below a cut are replay rows (0), the others fresh (1); the cut lies between 4 and 12.
All inputs are finite; a program needn't handle non-finite values.
Results may differ from the reference program's by a relative error of at most 0.0095.
Values may be sent and summed in bfloat16 or wider, within the bound.
A program may use at most 128 MiB of HBM per device.

```python
import jax
import jax.numpy as jnp
from jax import lax

D = 768
HEADS = 12
FF = 3072
HD = 64
L = 1024
ROWS_DEV = 2
ROWS = 16


def draw_segment_ids(key, part):
    key = jax.random.fold_in(key, 11)
    first_key, second_key = jax.random.split(key)
    border = max(L // 8, 2)
    opening = jax.random.randint(first_key, (ROWS, 1), 1, border + 1)
    closing = jax.random.randint(second_key, (ROWS, 1), L - border, L)
    position = jnp.arange(L)[None, :]
    return (position >= opening).astype(jnp.int32) + (position >= closing).astype(jnp.int32)


def draw_valid_mask(key, part):
    key = jax.random.fold_in(key, 23)
    devices_count = ROWS // ROWS_DEV
    owner = jnp.arange(ROWS) // ROWS_DEV
    denominator = max(3 * (devices_count - 1), 1)
    ceiling = L * (devices_count - 1 + 2 * owner) // denominator
    bottom = ceiling - ceiling // 4
    lengths = jax.random.randint(key, (ROWS,), bottom, ceiling + 1)
    position = jnp.arange(L)[None, :]
    return (position < lengths[:, None]).astype(jnp.int32)


def draw_row_half(key, part):
    key = jax.random.fold_in(key, 37)
    cutting = jax.random.randint(key, (), ROWS // 4, 3 * ROWS // 4 + 1)
    return (jnp.arange(ROWS) >= cutting).astype(jnp.int32)


def block_scale(stream_key, shape, shards, smallest, high):
    def one(dim, blocks):
        steps = jax.random.uniform(jax.random.fold_in(jax.random.fold_in(stream_key, 6), dim), (blocks,), jnp.float32, smallest / len(shards), high / len(shards))
        return jnp.repeat(jnp.exp(steps), shape[dim] // blocks).reshape((-1,) + (1,) * (len(shape) - dim - 1))

    loudness = one(*shards[0])
    for cut in shards[1:]:
        loudness = loudness * one(*cut)
    return loudness


def scatter_about(rng, extent, deviation, most, cuts=(), dtype=jnp.bfloat16):
    drawn = deviation * jax.random.normal(rng, extent, jnp.float32)
    if cuts:
        drawn = drawn * block_scale(rng, extent, cuts, -0.22, 0.18)
    return jnp.clip(drawn, -most, most).astype(dtype)


def setup_inputs(seed: int = 0) -> dict:
    key_list = jax.random.split(jax.random.key(seed), 18)
    return {
        "tokens": scatter_about(key_list[0], (ROWS, L, D), 1.0, 6.0, ((0, 8), (1, 4))),
        "cotangent": scatter_about(key_list[1], (ROWS, L, D), 1.0, 6.0, ((0, 8), (1, 4))),
        "segment_ids": draw_segment_ids(jax.random.fold_in(key_list[17], 71), 0),
        "valid_mask": draw_valid_mask(jax.random.fold_in(key_list[17], 71), 0),
        "row_half": draw_row_half(jax.random.fold_in(key_list[17], 71), 0),
        "norm1_gain": jnp.clip(1.0 + 0.1 * jax.random.normal(key_list[5], (D,), jnp.float32), 0.5, 1.5),
        "norm1_shift": scatter_about(key_list[6], (D,), 0.2, 1.0, (), jnp.float32),
        "qkv_weight": scatter_about(key_list[7], (D, 3, D), D ** -0.5, 0.21875, ((2, 4),)),
        "qkv_bias": scatter_about(key_list[8], (3, D), 0.2, 1.0, ((1, 4),), jnp.float32),
        "out_weight": scatter_about(key_list[9], (D, D), (max(D // 128, 1)) ** -0.5, 2.5, ((0, 4),)),
        "out_bias": scatter_about(key_list[10], (D,), 0.2, 1.0, (), jnp.float32),
        "norm2_gain": jnp.clip(1.0 + 0.1 * jax.random.normal(key_list[11], (D,), jnp.float32), 0.5, 1.5),
        "norm2_shift": scatter_about(key_list[12], (D,), 0.2, 1.0, (), jnp.float32),
        "fc_weight": scatter_about(key_list[13], (D, FF), D ** -0.5, 0.21875, ((1, 4),)),
        "fc_bias": scatter_about(key_list[14], (FF,), 0.2, 1.0, ((0, 4),), jnp.float32),
        "proj_weight": scatter_about(key_list[15], (FF, D), FF ** -0.5, 0.109375, ((0, 4),)),
        "proj_bias": scatter_about(key_list[16], (D,), 0.2, 1.0, (), jnp.float32),
    }


@jax.custom_vjp
def low(v):
    return lax.optimization_barrier(v.astype(jnp.bfloat16)).astype(jnp.float32)

@jax.custom_vjp
def low_back(v):
    return v

def low_keep(v):
    return (low(v), None)

def low_pass(kept, grad):
    return (grad,)

def back_keep(v):
    return (v, None)

def back_low(kept, grad):
    return (low(grad),)
low.defvjp(low_keep, low_pass)
low_back.defvjp(back_keep, back_low)
EPSILON = 1e-05
HIGHEST = lax.Precision.HIGHEST

def layer_norm(values, gain, shift):
    average = lax.optimization_barrier(jnp.mean(values, axis=-1, keepdims=True))
    centered = values - average
    spread = lax.optimization_barrier(jnp.mean(centered * centered, axis=-1, keepdims=True))
    return centered * lax.rsqrt(spread + EPSILON) * gain + shift

def smooth_gelu(values):
    return 0.5 * values * (1.0 + jnp.tanh(0.7978845608028654 * (values + 0.044715 * values * values * values)))

def one_row(params, row_values, segment_row):
    gain_one, shift_one, qkv_weight, qkv_bias, out_weight, out_bias, gain_two, shift_two, fc_weight, fc_bias, proj_weight, proj_bias = params
    normed = low(layer_norm(row_values, gain_one, shift_one))
    qkv = jnp.einsum('ld,dch->lch', normed, qkv_weight, precision=HIGHEST) + qkv_bias
    qkv = low(low_back(qkv))
    unpacked = qkv.reshape(L, 3, HEADS, HD)
    query_rows, key_rows, value_rows = (unpacked[:, 0], unpacked[:, 1], unpacked[:, 2])
    scores = jnp.einsum('qhd,khd->hqk', query_rows, key_rows, precision=HIGHEST) * HD ** (-0.5)
    scores = low_back(scores)
    position = jnp.arange(L)
    allowed = (position[None, :] <= position[:, None]) & (segment_row[None, :] == segment_row[:, None])
    scores = jnp.where(allowed[None], scores, -1e+30)
    maxima = lax.optimization_barrier(jnp.max(scores, axis=-1, keepdims=True))
    exponent = jnp.exp(scores - maxima)
    weights_low = low(exponent / lax.optimization_barrier(jnp.sum(exponent, axis=-1, keepdims=True)))
    attended = jnp.einsum('hqk,khd->qhd', weights_low, value_rows, precision=HIGHEST).reshape(L, D)
    attended = low(low_back(attended))
    branch = low_back(jnp.dot(attended, out_weight, precision=HIGHEST) + out_bias)
    middle = row_values + branch
    normed_two = low(layer_norm(middle, gain_two, shift_two))
    hidden = low_back(jnp.dot(normed_two, fc_weight, precision=HIGHEST) + fc_bias)
    hidden = low(smooth_gelu(hidden))
    branch_two = low_back(jnp.dot(hidden, proj_weight, precision=HIGHEST) + proj_bias)
    return middle + branch_two

def reference(tokens, cotangent, segment_ids, valid_mask, row_half, norm1_gain, norm1_shift, qkv_weight, qkv_bias, out_weight, out_bias, norm2_gain, norm2_shift, fc_weight, fc_bias, proj_weight, proj_bias):
    params = tuple((item.astype(jnp.float32) for item in (norm1_gain, norm1_shift, qkv_weight, qkv_bias, out_weight, out_bias, norm2_gain, norm2_shift, fc_weight, fc_bias, proj_weight, proj_bias)))
    rows_float = tokens.astype(jnp.float32)
    groups = ROWS // 4
    segment_groups = segment_ids.reshape(groups, 4, L)

    def forward(row_values, weights):

        def group_fn(bundle):
            return jax.vmap(lambda values, segment: one_row(weights, values, segment))(bundle[0], bundle[1])
        blocks = lax.map(jax.checkpoint(group_fn), (row_values.reshape(groups, 4, L, D), segment_groups))
        return blocks.reshape(ROWS, L, D)
    result, backward = jax.vjp(forward, rows_float, params)
    valid_float = valid_mask.astype(jnp.float32)
    row_counts = lax.optimization_barrier(jnp.sum(valid_float, axis=1))
    replay_count = jnp.sum(jnp.where(row_half == 0, row_counts, jnp.float32(0.0)))
    fresh_count = jnp.sum(jnp.where(row_half == 1, row_counts, jnp.float32(0.0)))
    row_scale = (replay_count + fresh_count) / (2.0 * jnp.where(row_half == 0, replay_count, fresh_count))
    out_grad = cotangent.astype(jnp.float32) * (valid_float * row_scale[:, None])[..., None]
    tokens_grad, grads = backward(out_grad)
    return (result.astype(jnp.bfloat16), tokens_grad, grads[0], grads[1], grads[2], grads[3], grads[4], grads[5], grads[6], grads[7], grads[8], grads[9], grads[10], grads[11])
```

```python
import functools

import jax
import jax.numpy as jnp
from jax import lax
from jax.experimental import pallas as pl
from jax.experimental.pallas import tpu as pltpu
from jax.sharding import PartitionSpec as P

HD = 64
EPSILON = 1e-05
SCALE = HD ** (-0.5)
EXP2_SCALE = SCALE * 1.4426950408889634
BLOCK = 256
F32 = jnp.float32
BF16 = jnp.bfloat16
NN = (((1,), (0,)), ((), ()))
NT = (((1,), (1,)), ((), ()))
TN = (((0,), (0,)), ((), ()))


def dot(a, b, dims=NN):
    return lax.dot_general(a, b, dims, preferred_element_type=F32)


def layer_norm(values, gain, shift):
    average = jnp.mean(values, axis=-1, keepdims=True)
    centered = values - average
    spread = jnp.mean(centered * centered, axis=-1, keepdims=True)
    return centered * lax.rsqrt(spread + EPSILON) * gain + shift


def smooth_gelu(values):
    return (
        0.5
        * values
        * (1.0 + jnp.tanh(0.7978845608028654 * (values + 0.044715 * values * values * values)))
    )


def attend_kernel(q_ref, k_ref, v_ref, seg_col_ref, seg_row_ref, p_ref, o_ref, inv_ref):
    heads, length, _ = q_ref.shape

    def head(h, _):
        for start in range(0, length, BLOCK):
            stop = start + BLOCK
            rows = slice(start, stop)
            scores = dot(q_ref[h, rows, :], k_ref[h, :stop, :], NT) * EXP2_SCALE
            query_at = start + lax.broadcasted_iota(jnp.int32, (BLOCK, stop), 0)
            key_at = lax.broadcasted_iota(jnp.int32, (BLOCK, stop), 1)
            allowed = (key_at <= query_at) & (seg_col_ref[rows, :] == seg_row_ref[:, :stop])
            scores = jnp.where(allowed, scores, -1e30)
            top = jnp.max(scores, axis=1, keepdims=True)
            exponent = jnp.exp2(scores - top)
            inverse = 1.0 / jnp.sum(exponent, axis=1, keepdims=True)
            low = exponent.astype(BF16)
            p_ref[h, rows, :stop] = low
            inv_ref[h, rows, :] = inverse
            o_ref[h, rows, :] = (dot(low, v_ref[h, :stop, :]) * inverse).astype(BF16)
        return 0

    lax.fori_loop(0, heads, head, 0)


def attend_back_kernel(
    q_ref, k_ref, v_ref, p_ref, o_ref, inv_ref, do_ref, dq_ref, dk_ref, dv_ref, key_acc, value_acc
):
    heads, length, _ = q_ref.shape

    def head(h, _):
        query_t = q_ref[h].T
        for start in range(0, length, BLOCK):
            stop = start + BLOCK
            rows = slice(start, stop)
            weights = p_ref[h, rows, :stop]
            upstream = (do_ref[h, rows, :] * inv_ref[h, rows, :]).astype(BF16)
            row_dot = jnp.sum(
                upstream.astype(F32) * o_ref[h, rows, :].astype(F32), axis=1, keepdims=True
            )
            weight_grad = dot(upstream, v_ref[h, :stop, :], NT)
            score_grad = (weights.astype(F32) * (weight_grad - row_dot)).astype(BF16)
            dq_ref[h, rows, :] = (dot(score_grad, k_ref[h, :stop, :]) * SCALE).astype(BF16)
            key_part = dot(query_t[:, rows], score_grad)
            value_part = dot(upstream.T, weights)
            if start:
                key_acc[:, :start] += key_part[:, :start]
                value_acc[:, :start] += value_part[:, :start]
            key_acc[:, rows] = key_part[:, start:]
            value_acc[:, rows] = value_part[:, start:]
        dk_ref[h] = (key_acc[...] * SCALE).T.astype(BF16)
        dv_ref[h] = value_acc[...].T.astype(BF16)
        return 0

    lax.fori_loop(0, heads, head, 0)


VMEM = pl.BlockSpec(memory_space=pltpu.VMEM)


def attend(q, k, v, segments):
    heads, length, _ = q.shape
    return pl.pallas_call(
        attend_kernel,
        out_shape=(
            jax.ShapeDtypeStruct((heads, length, length), BF16),
            jax.ShapeDtypeStruct((heads, length, HD), BF16),
            jax.ShapeDtypeStruct((heads, length, 1), F32),
        ),
        in_specs=[VMEM] * 5,
        out_specs=(VMEM,) * 3,
        compiler_params=pltpu.CompilerParams(vmem_limit_bytes=56 << 20),
    )(q, k, v, segments[:, None], segments[None, :])


def attend_back(q, k, v, p, o, inverse, upstream):
    heads, length, _ = q.shape
    shape = jax.ShapeDtypeStruct((heads, length, HD), BF16)
    return pl.pallas_call(
        attend_back_kernel,
        out_shape=(shape,) * 3,
        in_specs=[VMEM] * 7,
        out_specs=(VMEM,) * 3,
        scratch_shapes=[pltpu.VMEM((HD, length), F32)] * 2,
        compiler_params=pltpu.CompilerParams(vmem_limit_bytes=56 << 20),
    )(q, k, v, p, o, inverse, upstream)


def local(
    tokens,
    cotangent,
    segment_ids,
    valid_mask,
    row_half,
    norm1_gain,
    norm1_shift,
    qkv_weight,
    qkv_bias,
    out_weight,
    out_bias,
    norm2_gain,
    norm2_shift,
    fc_weight,
    fc_bias,
    proj_weight,
    proj_bias,
):
    place = lax.axis_index("tp")
    chip = place // 2
    core = place % 2
    owned, width = tokens.shape[1], tokens.shape[2]
    own_heads = out_weight.shape[0] // HD
    heads = 2 * own_heads

    def swap_chip(value):
        return lax.ppermute(value, "tp", [(i, i ^ 2) for i in range(4)])

    def swap_core(value):
        return lax.ppermute(value, "tp", [(i, i ^ 1) for i in range(4)])

    def row_pair(value):
        keep = jnp.where(chip == 0, value[0], value[1])
        got = swap_chip(jnp.where(chip == 0, value[1], value[0]))
        return jnp.where(chip == 0, jnp.stack([keep, got]), jnp.stack([got, keep]))

    def row_unpair(value):
        keep = jnp.where(chip == 0, value[0], value[1])
        got = swap_chip(jnp.where(chip == 0, value[1], value[0]))
        return jnp.where(chip == 0, jnp.stack([keep, got]), jnp.stack([got, keep]))

    def gather(value):
        other = swap_core(value)
        pairs = jnp.where(
            core == 0, jnp.stack([value, other], 1), jnp.stack([other, value], 1)
        )
        return pairs.reshape((4 * owned,) + value.shape[2:])

    def scatter(value):
        parts = value.reshape(2, 2, owned, width)
        keep = jnp.where(core == 0, parts[:, 0], parts[:, 1])
        give = jnp.where(core == 0, parts[:, 1], parts[:, 0])
        return keep + swap_core(give)

    other_qkv = swap_chip(qkv_weight)
    other_out = swap_chip(out_weight)
    other_fc = swap_chip(fc_weight)
    other_proj = swap_chip(proj_weight)
    qkv_all = jnp.concatenate([qkv_weight, other_qkv], axis=2)
    out_all = jnp.concatenate([out_weight, other_out], axis=0)
    fc_all = jnp.concatenate([fc_weight, other_fc], axis=1)
    proj_all = jnp.concatenate([proj_weight, other_proj], axis=0)
    qkv_bias_all = jnp.concatenate([qkv_bias, swap_chip(qkv_bias)], axis=1)
    fc_bias_all = jnp.concatenate([fc_bias, swap_chip(fc_bias)], axis=0)

    valid_float = valid_mask.astype(F32)
    row_counts = jnp.sum(valid_float, axis=1)
    replay_local = jnp.sum(jnp.where(row_half == 0, row_counts, 0.0))
    fresh_local = jnp.sum(jnp.where(row_half == 1, row_counts, 0.0))
    replay_count, fresh_count = lax.psum((replay_local, fresh_local), ("dp", "tp"))
    row_scale = (replay_count + fresh_count) / (
        2.0 * jnp.where(row_half == 0, replay_count, fresh_count)
    )
    my_scale = jnp.where(chip == 0, row_scale[0], row_scale[1])

    rows = row_pair(tokens).astype(F32)
    segments = gather(row_pair(segment_ids))
    valid = row_pair(valid_float)
    normed, norm1_back = jax.vjp(layer_norm, rows, norm1_gain, norm1_shift)
    full_normed = gather(normed.astype(BF16))
    qkv = jnp.einsum(
        "ld,dchk->chlk",
        full_normed,
        qkv_all.reshape(width, 3, heads, HD),
        preferred_element_type=F32,
    ) + qkv_bias_all.reshape(3, heads, 1, HD)
    qkv_low = qkv.astype(BF16)
    weights, mixed, inverse = attend(qkv_low[0], qkv_low[1], qkv_low[2], segments)
    out_split = out_all.reshape(heads, HD, width)
    attn = scatter(
        jnp.einsum("hlk,hkd->ld", mixed, out_split, preferred_element_type=F32)
    )
    middle = rows + attn + out_bias
    normed_two, norm2_back = jax.vjp(layer_norm, middle, norm2_gain, norm2_shift)
    full_normed_two = gather(normed_two.astype(BF16))
    hidden_pre = jnp.dot(full_normed_two, fc_all, preferred_element_type=F32) + fc_bias_all
    hidden_act, gelu_back = jax.vjp(smooth_gelu, hidden_pre)
    hidden_low = hidden_act.astype(BF16)
    mlp = scatter(jnp.dot(hidden_low, proj_all, preferred_element_type=F32))
    result = middle + mlp + proj_bias
    output = row_unpair(result.astype(BF16))

    out_grad = row_pair(cotangent).astype(F32) * (valid * my_scale)[..., None]
    branch_low = out_grad.astype(BF16)
    proj_bias_grad = jnp.sum(branch_low, axis=(0, 1), dtype=F32)
    full_grad = gather(branch_low)
    hidden_grad = dot(full_grad, proj_all, NT)
    proj_weight_grad = dot(hidden_low, full_grad, TN)
    (pre_grad,) = gelu_back(hidden_grad)
    pre_low = pre_grad.astype(BF16)
    fc_bias_grad = jnp.sum(pre_low, axis=0, dtype=F32)
    fc_weight_grad = dot(full_normed_two, pre_low, TN)
    normed_two_grad = scatter(dot(pre_low, fc_all, NT))
    middle_part, norm2_gain_grad, norm2_shift_grad = norm2_back(normed_two_grad)
    middle_grad = out_grad + middle_part
    attn_low = middle_grad.astype(BF16)
    out_bias_grad = jnp.sum(attn_low, axis=(0, 1), dtype=F32)
    full_attn_grad = gather(attn_low)
    mixed_grad = jnp.einsum("ld,hkd->hlk", full_attn_grad, out_split, preferred_element_type=F32)
    out_weight_grad = jnp.einsum(
        "hlk,ld->hkd", mixed, full_attn_grad, preferred_element_type=F32
    ).reshape(heads * HD, width)
    query_grad, key_grad, value_grad = attend_back(
        qkv_low[0], qkv_low[1], qkv_low[2], weights, mixed, inverse, mixed_grad
    )
    qkv_grad = jnp.stack([query_grad, key_grad, value_grad])
    qkv_bias_grad = jnp.sum(qkv_grad, axis=2, dtype=F32).reshape(3, heads * HD)
    qkv_weight_grad = jnp.einsum(
        "ld,chlk->dchk", full_normed, qkv_grad, preferred_element_type=F32
    ).reshape(width, 3, heads * HD)
    normed_grad = scatter(
        jnp.einsum(
            "chlk,dchk->ld",
            qkv_grad,
            qkv_all.reshape(width, 3, heads, HD),
            preferred_element_type=F32,
        )
    )
    tokens_part, norm1_gain_grad, norm1_shift_grad = norm1_back(normed_grad)
    tokens_grad = row_unpair(middle_grad + tokens_part)

    (
        norm1_gain_grad,
        norm1_shift_grad,
        norm2_gain_grad,
        norm2_shift_grad,
        out_bias_grad,
        proj_bias_grad,
    ) = lax.psum(
        (
            norm1_gain_grad,
            norm1_shift_grad,
            norm2_gain_grad,
            norm2_shift_grad,
            out_bias_grad,
            proj_bias_grad,
        ),
        ("dp", "tp"),
    )

    def reduce_weight(value, axis, low=True):
        size = value.shape[axis] // 2
        mine = lax.slice_in_dim(value, 0, size, axis=axis)
        other = lax.slice_in_dim(value, size, 2 * size, axis=axis)
        if low:
            total = mine + swap_chip(other.astype(BF16)).astype(F32)
            return lax.psum(total.astype(BF16), "dp").astype(F32)
        return lax.psum(mine + swap_chip(other), "dp")

    return (
        output,
        tokens_grad,
        norm1_gain_grad,
        norm1_shift_grad,
        reduce_weight(qkv_weight_grad, 2),
        reduce_weight(qkv_bias_grad, 1, False),
        reduce_weight(out_weight_grad, 0),
        out_bias_grad,
        norm2_gain_grad,
        norm2_shift_grad,
        reduce_weight(fc_weight_grad, 1),
        reduce_weight(fc_bias_grad, 0, False),
        reduce_weight(proj_weight_grad, 0),
        proj_bias_grad,
    )


def solution(mesh):
    in_specs = (
        P("dp", "tp", None),
        P("dp", "tp", None),
        P("dp", "tp"),
        P("dp", "tp"),
        P("dp"),
        P(),
        P(),
        P(None, None, "tp"),
        P(None, "tp"),
        P("tp", None),
        P(),
        P(),
        P(),
        P(None, "tp"),
        P("tp"),
        P("tp", None),
        P(),
    )
    out_specs = (
        P("dp", "tp", None),
        P("dp", "tp", None),
        P(),
        P(),
        P(None, None, "tp"),
        P(None, "tp"),
        P("tp", None),
        P(),
        P(),
        P(),
        P(None, "tp"),
        P("tp"),
        P("tp", None),
        P(),
    )
    return jax.shard_map(local, mesh=mesh, in_specs=in_specs, out_specs=out_specs, check_vma=False)
```

```python
import functools

import jax
import jax.numpy as jnp
from jax import lax
from jax.experimental import pallas as pl
from jax.experimental.pallas import tpu as pltpu
from jax.sharding import PartitionSpec as P

HD = 64
EPSILON = 1e-05
SCALE = HD ** (-0.5)
EXP2_SCALE = SCALE * 1.4426950408889634
GELU_A = 0.7978845608028654
GELU_B = 0.044715
T = 256
F32 = jnp.float32
BF16 = jnp.bfloat16
NN = (((1,), (0,)), ((), ()))
NT = (((1,), (1,)), ((), ()))
TN = (((0,), (0,)), ((), ()))
MESH = pl.DeviceIdType.MESH
GROUP = 8


def dot(a, b, dims=NN):
    return lax.dot_general(a, b, dims, preferred_element_type=F32)


def sub_rows(base, size, chunk, body):
    def step(i, carry):
        body(pl.ds(pl.multiple_of(base + i * chunk, chunk), chunk), i * chunk)
        return carry

    lax.fori_loop(0, size // chunk, step, 0)


class Links:
    def __init__(self, send_sems, recv_sems):
        self.send_sems, self.recv_sems = send_sems, recv_sems
        self.copies = []
        self.sent = []

    def send(self, source, target, device):
        index = len(self.copies)
        copy = pltpu.make_async_remote_copy(
            src_ref=source,
            dst_ref=target,
            send_sem=self.send_sems.at[index],
            recv_sem=self.recv_sems.at[index],
            device_id=device,
            device_id_type=MESH,
        )
        copy.start()
        self.copies.append(copy)
        return copy

    def wait_send(self, copy):
        copy.wait_send()
        self.sent.append(copy)

    def finish(self):
        for copy in self.copies:
            if not any(copy is other for other in self.sent):
                copy.wait_send()


def layer_kernel(
    dp_size,
    tok_ref,
    cot_ref,
    info_ref,
    vec_ref,
    bias_ref,
    wqkv_ref,
    wout_ref,
    wfc_ref,
    wproj_ref,
    out_ref,
    tgrad_ref,
    dproj_ref,
    dfc_ref,
    dattn_ref,
    small_ref,
    tok_in,
    cot_in,
    info_buf,
    bias_in,
    wqkv_in,
    wout_all,
    wfc_in,
    wproj_in,
    count_out,
    count_in,
    seg_col,
    weight_col,
    normed,
    normed2,
    grad_full,
    attn_grad,
    q_s,
    k_s,
    v_s,
    o_s,
    do_s,
    p0,
    p1,
    p2,
    p3,
    att,
    middle,
    hid,
    dpre,
    give,
    got,
    own,
    give2,
    got2,
    key_acc,
    value_acc,
    acc_half,
    acc_attn,
    x_give,
    x_got,
    y_got,
    z_got,
    out_give,
    tg_give,
    tg_got,
    small_a,
    small_in,
    small_b,
    small_dp,
    send_sems,
    recv_sems,
    local_sems,
):
    d = lax.axis_index("dp")
    t = lax.axis_index("tp")
    x = t // 2
    c = t - 2 * x
    t_core = t + 1 - 2 * c
    t_chip = lax.rem(t + 2, 4)
    t_both = 3 - t
    y = lax.rem(d, 2)
    group_first = d - lax.rem(d, GROUP)
    place = d - group_first
    z = place // 2
    d_y = d + 1 - 2 * y

    def d_flip(bit):
        size = 1 << bit
        return d + size - 2 * size * lax.rem(d // size, 2)

    def d_z(step):
        return group_first + 2 * lax.rem(z + step, 4) + y

    dqkv = hid
    count_bits = dp_size.bit_length() - 1
    links = Links(send_sems, recv_sems)
    send = links.send

    barrier = pltpu.get_barrier_semaphore()
    peers = [(d, t_core), (d, t_chip), (d, t_both)]
    peers += [(group_first + lax.rem(place + k, GROUP), t) for k in range(1, GROUP)]
    peers += [(d_flip(bit), t) for bit in range(3, count_bits)]
    for peer in peers:
        pl.semaphore_signal(barrier, inc=1, device_id=peer, device_id_type=MESH)
    pl.semaphore_wait(barrier, len(peers))

    def block_rows(index):
        return pl.ds(pl.multiple_of(index * T, T), T)

    gain1, shift1, out_bias = vec_ref[0:1, :], vec_ref[1:2, :], vec_ref[2:3, :]
    gain2, shift2, proj_bias = vec_ref[3:4, :], vec_ref[4:5, :], vec_ref[5:6, :]

    tok_copy = send(tok_ref.at[1 - x], tok_in, (d, t_chip))
    info_buf[t] = info_ref[x]
    info_copies = [
        send(info_ref.at[x], info_buf.at[t], (d, t_core)),
        send(info_ref.at[1 - x], info_buf.at[t], (d, t_chip)),
        send(info_ref.at[1 - x], info_buf.at[t], (d, t_both)),
    ]
    bias_copy = send(bias_ref, bias_in, (d, t_chip))
    wout_all[0:192, :] = wout_ref[...]
    for ref in (small_a, count_out):
        ref[...] = jnp.zeros_like(ref)

    def moments(values):
        average = jnp.mean(values, axis=-1, keepdims=True)
        centered = values - average
        spread = jnp.mean(centered * centered, axis=-1, keepdims=True)
        inverse = lax.rsqrt(spread + EPSILON)
        return centered * inverse, inverse

    def norm_one(load, index):
        base = index * T

        def body(rows, at):
            scaled, _ = moments(load(at))
            normed[rows, :] = (scaled * gain1 + shift1).astype(BF16)

        sub_rows(base, T, 64, body)

    def tok_own(at):
        return tok_ref[x, pl.ds(at, 64), :].astype(F32)

    def tok_other(at):
        return tok_in[pl.ds(at, 64), :].astype(F32)

    norm_one(tok_own, t)
    normed_copies = [send(normed.at[block_rows(t)], normed.at[block_rows(t)], (d, t_core))]
    tok_copy.wait_recv()
    wqkv_half = pl.ds(pl.multiple_of(y * 288, 16), 288)
    wout_half = pl.ds(pl.multiple_of(y * 96, 16), 96)
    wout_half_in = pl.ds(pl.multiple_of(192 + y * 96, 16), 96)
    w_half = pl.ds(pl.multiple_of(y * 384, 16), 384)
    wqkv_x = send(wqkv_ref.at[wqkv_half], wqkv_in.at[wqkv_half], (d, t_chip))
    wout_x = send(wout_ref.at[wout_half], wout_all.at[wout_half_in], (d, t_chip))
    norm_one(tok_other, t_chip)
    normed_copies.append(
        send(normed.at[block_rows(t_chip)], normed.at[block_rows(t_chip)], (d, t_core))
    )
    for copy in info_copies:
        copy.wait_recv()

    half = info_buf[0, 2:3, 0:1]
    count = jnp.sum(info_buf[0, 1:2, :], axis=1, keepdims=True)
    for index in range(1, 4):
        count = count + jnp.sum(info_buf[index, 1:2, :], axis=1, keepdims=True)
    counts = [count * (1.0 - half), count * half]
    count_peers = [(d, t_chip)] + [(d_flip(bit), t) for bit in range(count_bits)]
    count_copies = []

    def count_start():
        step = len(count_copies)
        if step < len(count_peers):
            count_out[step, 0:1, :] = jnp.broadcast_to(counts[0], (1, 128))
            count_out[step, 1:2, :] = jnp.broadcast_to(counts[1], (1, 128))
            count_copies.append(send(count_out.at[step], count_in.at[step], count_peers[step]))

    def count_end():
        step = len(count_copies) - 1
        count_copies[step].wait_recv()
        counts[0] = counts[0] + count_in[step, 0:1, 0:1]
        counts[1] = counts[1] + count_in[step, 1:2, 0:1]

    count_start()
    seg_row = jnp.concatenate([info_buf[i, 0:1, :] for i in range(4)], axis=1)
    for index in range(4):
        row = jnp.broadcast_to(info_buf[index, 0:1, :], (128, T))
        seg_col[index * T : (index + 1) * T, :] = row.T
    for copy in normed_copies:
        copy.wait_recv()

    def project(side, weight):
        bias = (bias_ref if side == 0 else bias_in)[1:2, 0:576]

        def body(rows, at):
            value = (dot(normed[rows, :], weight[...], NT) + bias).astype(BF16)
            for part, ref in enumerate((q_s, k_s, v_s)):
                for h in range(3):
                    lane = part * 192 + h * HD
                    ref[3 * side + h, rows, :] = value[:, lane : lane + HD]

        sub_rows(0, 4 * T, T, body)

    p_refs = (p0, p1, p2, p3)

    def attend(side):
        def head(h, carry):
            for index, p_ref in enumerate(p_refs):
                start, stop = index * T, (index + 1) * T
                rows = slice(start, stop)
                scores = dot(q_s[h, rows, :], k_s[h, 0:stop, :], NT) * EXP2_SCALE
                query_at = start + lax.broadcasted_iota(jnp.int32, (T, stop), 0)
                key_at = lax.broadcasted_iota(jnp.int32, (T, stop), 1)
                allowed = (key_at <= query_at) & (seg_col[rows, 0:1] == seg_row[:, 0:stop])
                scores = jnp.where(allowed, scores, -1e30)
                top = jnp.max(scores, axis=1, keepdims=True)
                exponent = jnp.exp2(scores - top)
                inverse = 1.0 / jnp.sum(exponent, axis=1, keepdims=True)
                low = (exponent * inverse).astype(BF16)
                p_ref[h] = low
                o_s[h, rows, :] = dot(low, v_s[h, 0:stop, :]).astype(BF16)
            return carry

        lax.fori_loop(3 * side, 3 * side + 3, head, 0)

    project(0, wqkv_ref)
    attend(0)
    count_end()
    count_start()
    wqkv_x.wait_recv()
    wqkv_y = send(wqkv_in.at[wqkv_half], wqkv_in.at[wqkv_half], (d_y, t))
    wout_x.wait_recv()
    wout_y = send(wout_all.at[wout_half_in], wout_all.at[wout_half_in], (d_y, t))
    cot_copy = send(cot_ref.at[1 - x], cot_in, (d, t_chip))
    wfc_x = send(wfc_ref.at[w_half], wfc_in.at[w_half], (d, t_chip))
    bias_copy.wait_recv()
    wqkv_y.wait_recv()
    project(1, wqkv_in)
    wproj_x = send(wproj_ref.at[w_half], wproj_in.at[w_half], (d, t_chip))
    attend(1)
    count_end()
    count_start()
    for h in range(6):
        att[:, h * HD : (h + 1) * HD] = o_s[h]

    def scatter(partial, give_ref, got_ref, before=()):
        for copy in before:
            links.wait_send(copy)
        copies = []
        for slot, index in enumerate((t_core, t_both)):
            give_ref[slot] = partial(index).astype(BF16)
            copies.append(send(give_ref.at[slot], got_ref.at[slot], (d, t_core)))
        for slot, index in enumerate((t, t_chip)):
            own[slot] = partial(index)
        return copies

    def out_partial(index):
        return dot(att[block_rows(index), :], wout_all[...])

    wout_y.wait_recv()
    attn_copies = scatter(out_partial, give, got)
    wfc_x.wait_recv()
    wfc_y = send(wfc_in.at[w_half], wfc_in.at[w_half], (d_y, t))
    count_end()
    count_start()

    normed2_copies = []
    for slot, index in enumerate((t, t_chip)):
        attn_copies[slot].wait_recv()
        load = tok_own if slot == 0 else tok_other

        def body(rows, at, slot=slot, index=index, load=load):
            value = load(at) + own[slot, rows, :] + got[slot, rows, :].astype(F32) + out_bias
            middle[slot, rows, :] = value
            scaled, _ = moments(value)
            normed2[pl.ds(pl.multiple_of(index * T + at, 64), 64), :] = (
                scaled * gain2 + shift2
            ).astype(BF16)

        sub_rows(0, T, 64, body)
        rows = block_rows(index)
        normed2_copies.append(send(normed2.at[rows], normed2.at[rows], (d, t_core)))
    while len(count_copies) < len(count_peers):
        count_end()
        count_start()
    count_end()

    row_scale = (counts[0] + counts[1]) / (2.0 * jnp.where(half == 0.0, counts[0], counts[1]))
    cot_copy.wait_recv()
    grad_copies = []
    for slot, index in enumerate((t, t_chip)):
        row = jnp.broadcast_to(info_buf[index, 1:2, :] * row_scale, (128, T))
        weight_col[slot] = row.T

    def out_grad(slot, rows, at):
        source = cot_ref[x, rows, :] if slot == 0 else cot_in[rows, :]
        return source.astype(F32) * weight_col[slot, rows, 0:1]

    for slot, index in enumerate((t, t_chip)):

        def body(rows, at, slot=slot, index=index):
            low = out_grad(slot, rows, at).astype(BF16)
            grad_full[pl.ds(pl.multiple_of(index * T + at, 64), 64), :] = low
            small_a[0, 5:6, :] += jnp.sum(low.astype(F32), axis=0, keepdims=True)

        sub_rows(0, T, 64, body)
        rows = block_rows(index)
        grad_copies.append(send(grad_full.at[rows], grad_full.at[rows], (d, t_core)))
    for copy in normed2_copies + grad_copies:
        copy.wait_recv()

    def mlp(side, fc, proj):
        bias = (bias_ref if side == 0 else bias_in)[0:1, :]

        def body(rows, at):
            pre = dot(normed2[rows, :], fc[...]) + bias
            square = pre * pre
            bent = jnp.tanh(GELU_A * (pre + GELU_B * square * pre))
            rise = 0.5 * (1.0 + bent)
            hid[side, rows, :] = (pre * rise).astype(BF16)
            slope = rise + 0.5 * pre * (1.0 - bent * bent) * (
                GELU_A + (3.0 * GELU_A * GELU_B) * square
            )
            low = (dot(grad_full[rows, :], proj[...], NT) * slope).astype(BF16)
            dpre[side, rows, :] = low
            small_a[0, 6 + 2 * side : 7 + 2 * side, :] += jnp.sum(
                low.astype(F32), axis=0, keepdims=True
            )

        sub_rows(0, 4 * T, T, body)

    mlp(0, wfc_ref, wproj_ref)
    wproj_x.wait_recv()
    wproj_y = send(wproj_in.at[w_half], wproj_in.at[w_half], (d_y, t))
    wfc_y.wait_recv()
    wproj_y.wait_recv()
    mlp(1, wfc_in, wproj_in)

    def weight_rows(body):
        sub_rows(0, 768, T, lambda rows, at: body(rows))

    def x_start(m, product):
        def body(rows):
            x_give[m, rows, :] = product(rows).astype(BF16)

        weight_rows(body)
        return send(x_give.at[m], x_got.at[m], (d, t_chip))

    def half_rows(index):
        return pl.ds(pl.multiple_of(index * 384, 384), 384)

    def y_start(m, product):
        other, mine = half_rows(1 - y), half_rows(y)
        x_got[m, other, :] = (product(other) + x_got[m, other, :].astype(F32)).astype(BF16)
        copy = send(x_got.at[m, other], y_got.at[m], (d_y, t))
        acc_half[m] = product(mine) + x_got[m, mine, :].astype(F32)
        return copy

    def quarter(index):
        return pl.ds(pl.multiple_of(index * 96, 96), 96)

    def quarter_sum(m, index):
        local = quarter(index)
        if m == 2:
            mine = acc_attn[pl.ds(pl.multiple_of(y * 384 + index * 96, 96), 96), :]
        else:
            mine = acc_half[m, local, :]
        return mine + y_got[m, local, :].astype(F32)

    def z_start(m):
        copies = []
        for step in range(1, 4):
            rows = quarter(lax.rem(z + step, 4))
            y_got[m, rows, :] = quarter_sum(m, lax.rem(z + step, 4)).astype(BF16)
            copies.append(send(y_got.at[m, rows], z_got.at[m, step - 1], (d_z(step), t)))
        return copies

    weight_outs = (dproj_ref, dfc_ref, dattn_ref)

    def z_end(m):
        total = quarter_sum(m, z)
        for step in range(3):
            total = total + z_got[m, step].astype(F32)
        y_got[m, quarter(z), :] = total.astype(BF16)
        fin = y_got.at[m, quarter(z)]
        rows = pl.ds(pl.multiple_of(y * 384 + z * 96, 96), 96)
        keep = pltpu.make_async_copy(fin, weight_outs[m].at[rows], local_sems.at[m])
        keep.start()
        spread = [send(fin, weight_outs[m].at[rows], (d_z(step), t)) for step in range(1, 4)]
        across = [send(fin, weight_outs[m].at[rows], (d_y, t))]
        return keep, spread, across

    def spread_on(m, state):
        _, spread, across = state
        for step in range(1, 4):
            spread[step - 1].wait_recv()
            source = lax.rem(z + 4 - step, 4)
            rows = pl.ds(pl.multiple_of(y * 384 + source * 96, 96), 96)
            across.append(send(weight_outs[m].at[rows], weight_outs[m].at[rows], (d_y, t)))

    def spread_end(state):
        keep, _, across = state
        keep.wait()
        for copy in across:
            copy.wait_recv()

    def proj_product(side):
        return lambda rows: dot(hid[side, :, rows], grad_full[...], TN)

    def fc_product(side):
        return lambda rows: dot(normed2[:, rows], dpre[side], TN)

    proj_x = x_start(0, proj_product(1))
    fc_x = x_start(1, fc_product(1))

    def mlp_partial(index):
        rows = block_rows(index)
        return dot(hid[0, rows, :], wproj_ref[...]) + dot(hid[1, rows, :], wproj_in[...])

    mlp_copies = scatter(mlp_partial, give2, got2)
    for slot in range(2):
        mlp_copies[slot].wait_recv()

        def body(rows, at, slot=slot):
            value = (
                middle[slot, rows, :]
                + own[slot, rows, :]
                + got2[slot, rows, :].astype(F32)
                + proj_bias
            )
            if slot == 0:
                out_ref[x, rows, :] = value.astype(BF16)
            else:
                out_give[rows, :] = value.astype(BF16)

        sub_rows(0, T, 64, body)
    out_copy = send(out_give, out_ref.at[x], (d, t_chip))

    def norm2_partial(index):
        rows = block_rows(index)
        return dot(dpre[0, rows, :], wfc_ref[...], NT) + dot(dpre[1, rows, :], wfc_in[...], NT)

    back_copies = scatter(norm2_partial, give, got, attn_copies)
    def norm_back(upstream, values, gain):
        scaled, inverse = moments(values)
        pushed = upstream * gain
        mean_one = jnp.mean(pushed, axis=-1, keepdims=True)
        mean_two = jnp.mean(pushed * scaled, axis=-1, keepdims=True)
        gain_grad = jnp.sum(upstream * scaled, axis=0, keepdims=True)
        shift_grad = jnp.sum(upstream, axis=0, keepdims=True)
        return inverse * (pushed - mean_one - scaled * mean_two), gain_grad, shift_grad

    grad_copies = []
    for slot, index in enumerate((t, t_chip)):
        back_copies[slot].wait_recv()

        def body(rows, at, slot=slot, index=index):
            upstream = own[slot, rows, :] + got[slot, rows, :].astype(F32)
            part, gain_grad, shift_grad = norm_back(upstream, middle[slot, rows, :], gain2)
            value = out_grad(slot, rows, at) + part
            middle[slot, rows, :] = value
            low = value.astype(BF16)
            attn_grad[pl.ds(pl.multiple_of(index * T + at, 64), 64), :] = low
            small_a[0, 2:3, :] += gain_grad
            small_a[0, 3:4, :] += shift_grad
            small_a[0, 4:5, :] += jnp.sum(low.astype(F32), axis=0, keepdims=True)

        sub_rows(0, T, 64, body)
        rows = block_rows(index)
        grad_copies.append(send(attn_grad.at[rows], attn_grad.at[rows], (d, t_core)))
    for copy in grad_copies:
        copy.wait_recv()

    def spread_heads(rows, at):
        value = dot(attn_grad[rows, :], wout_all[...], NT)
        for h in range(6):
            do_s[h, rows, :] = value[:, h * HD : (h + 1) * HD].astype(BF16)

    sub_rows(0, 4 * T, T, spread_heads)
    x_give[2, 576:768, :] = dot(att[:, 192:384], attn_grad[...], TN).astype(BF16)
    out_x = send(x_give.at[2, 576:768], x_got.at[2, 576:768], (d, t_chip))
    acc_attn[576:768, :] = dot(att[:, 0:192], attn_grad[...], TN)
    proj_x.wait_recv()
    proj_y = y_start(0, proj_product(0))

    def attend_back(side):
        def head(h, carry):
            query_t = q_s[h].T
            for index, p_ref in enumerate(p_refs):
                start, stop = index * T, (index + 1) * T
                rows = slice(start, stop)
                weights = p_ref[h]
                upstream = do_s[h, rows, :]
                row_dot = jnp.sum(
                    upstream.astype(F32) * o_s[h, rows, :].astype(F32), axis=1, keepdims=True
                )
                weight_grad = dot(upstream, v_s[h, 0:stop, :], NT)
                score_grad = (weights.astype(F32) * (weight_grad - row_dot)).astype(BF16)
                q_s[h, rows, :] = (dot(score_grad, k_s[h, 0:stop, :]) * SCALE).astype(BF16)
                key_part = dot(query_t[:, rows], score_grad)
                value_part = dot(upstream.T, weights)
                if start:
                    key_acc[:, 0:start] += key_part[:, 0:start]
                    value_acc[:, 0:start] += value_part[:, 0:start]
                key_acc[:, rows] = key_part[:, start:]
                value_acc[:, rows] = value_part[:, start:]
            k_s[h] = (key_acc[...] * SCALE).T.astype(BF16)
            v_s[h] = value_acc[...].T.astype(BF16)
            return carry

        lax.fori_loop(3 * side, 3 * side + 3, head, 0)
        for part, ref in enumerate((q_s, k_s, v_s)):
            for h in range(3):
                lane = part * 192 + h * HD
                dqkv[side, :, lane : lane + HD] = ref[3 * side + h]
        small_a[0, 7 + 2 * side : 8 + 2 * side, 0:576] = jnp.sum(
            dqkv[side, :, 0:576].astype(F32), axis=0, keepdims=True
        )

    attend_back(1)
    for start in range(0, 576, 192):
        x_give[2, start : start + 192, :] = dot(
            dqkv[1, :, start : start + 192], normed[...], TN
        ).astype(BF16)
    qkv_x = send(x_give.at[2, 0:576], x_got.at[2, 0:576], (d, t_chip))

    proj_y.wait_recv()
    proj_z = z_start(0)
    fc_x.wait_recv()
    fc_y = y_start(1, fc_product(0))
    attend_back(0)

    def norm1_partial(index):
        rows = block_rows(index)
        return dot(dqkv[0, rows, 0:576], wqkv_ref[...]) + dot(dqkv[1, rows, 0:576], wqkv_in[...])

    back_copies = scatter(norm1_partial, give, got, back_copies)
    for copy in proj_z:
        copy.wait_recv()
    proj_state = z_end(0)
    fc_y.wait_recv()
    fc_z = z_start(1)
    for slot in (1, 0):
        back_copies[slot].wait_recv()
        load = tok_own if slot == 0 else tok_other

        def body(rows, at, slot=slot, load=load):
            upstream = own[slot, rows, :] + got[slot, rows, :].astype(F32)
            part, gain_grad, shift_grad = norm_back(upstream, load(at), gain1)
            value = middle[slot, rows, :] + part
            if slot == 0:
                own[0, rows, :] = value
            else:
                tg_give[rows, :] = value.astype(BF16)
            small_a[0, 0:1, :] += gain_grad
            small_a[0, 1:2, :] += shift_grad

        sub_rows(0, T, 64, body)
        if slot == 1:
            tg_copy = send(tg_give, tg_got, (d, t_chip))
    tg_keep = [pltpu.make_async_copy(own.at[0], tgrad_ref.at[x], local_sems.at[3])]
    tg_keep[0].start()

    small_copies = [
        send(small_a.at[0], small_in.at[0], (d, t_core)),
        send(small_a.at[0], small_in.at[1], (d, t_chip)),
        send(small_a.at[0], small_in.at[2], (d, t_both)),
    ]
    for start in range(0, 576, 192):
        acc_attn[start : start + 192, :] = dot(
            dqkv[0, :, start : start + 192], normed[...], TN
        )
    out_x.wait_recv()
    qkv_x.wait_recv()

    def add_received(rows):
        acc_attn[rows, :] += x_got[2, rows, :].astype(F32)

    weight_rows(add_received)
    x_got[2, half_rows(1 - y), :] = acc_attn[half_rows(1 - y), :].astype(BF16)
    attn_y = send(x_got.at[2, half_rows(1 - y)], y_got.at[2], (d_y, t))
    for copy in fc_z:
        copy.wait_recv()
    fc_state = z_end(1)
    spread_on(0, proj_state)

    for copy in small_copies:
        copy.wait_recv()
    small_b[0:6, :] = (
        small_a[0, 0:6, :] + small_in[0, 0:6, :] + small_in[1, 0:6, :] + small_in[2, 0:6, :]
    )
    small_b[6:8, :] = small_a[0, 6:8, :] + small_in[1, 8:10, :]
    small_dp_copies = [
        send(small_b, small_dp.at[k - 1], (group_first + lax.rem(place + k, GROUP), t))
        for k in range(1, GROUP)
    ]
    attn_y.wait_recv()
    attn_z = z_start(2)
    for copy in small_dp_copies:
        copy.wait_recv()
    total = small_b[...]
    for k in range(GROUP - 1):
        total = total + small_dp[k]
    small_ref[...] = total
    tg_copy.wait_recv()
    own[1] = tg_got[...].astype(F32)
    tg_keep.append(pltpu.make_async_copy(own.at[1], tgrad_ref.at[1 - x], local_sems.at[4]))
    tg_keep[1].start()
    spread_on(1, fc_state)
    for copy in attn_z:
        copy.wait_recv()
    attn_state = z_end(2)
    spread_on(2, attn_state)
    out_copy.wait_recv()
    for state in (proj_state, fc_state, attn_state):
        spread_end(state)
    for copy in tg_keep:
        copy.wait()
    links.finish()


VMEM = pl.BlockSpec(memory_space=pltpu.VMEM)
ANY = pl.BlockSpec(memory_space=pl.ANY)


def local(
    dp_size,
    tokens,
    cotangent,
    segment_ids,
    valid_mask,
    row_half,
    norm1_gain,
    norm1_shift,
    qkv_weight,
    qkv_bias,
    out_weight,
    out_bias,
    norm2_gain,
    norm2_shift,
    fc_weight,
    fc_bias,
    proj_weight,
    proj_bias,
):
    half_rows = jnp.broadcast_to(row_half[:, None], segment_ids.shape)
    empty = jnp.zeros_like(segment_ids)
    info = jnp.stack([segment_ids, valid_mask, half_rows] + [empty] * 5, axis=1).astype(F32)
    nothing = jnp.zeros_like(out_bias)
    vectors = jnp.stack(
        [norm1_gain, norm1_shift, out_bias, norm2_gain, norm2_shift, proj_bias, nothing, nothing]
    )
    flat_bias = jnp.concatenate([qkv_bias.reshape(576), jnp.zeros((192,), F32)])
    biases = jnp.stack([fc_bias, flat_bias] + [nothing] * 6)
    qkv_rows = jnp.transpose(qkv_weight, (1, 2, 0)).reshape(576, 768)

    copies = 128

    def buffer(shape, dtype):
        return pltpu.VMEM(shape, dtype)

    outs = pl.pallas_call(
        functools.partial(layer_kernel, dp_size),
        out_shape=(
            jax.ShapeDtypeStruct((2, T, 768), BF16),
            jax.ShapeDtypeStruct((2, T, 768), F32),
            jax.ShapeDtypeStruct((768, 768), BF16),
            jax.ShapeDtypeStruct((768, 768), BF16),
            jax.ShapeDtypeStruct((768, 768), BF16),
            jax.ShapeDtypeStruct((8, 768), F32),
        ),
        in_specs=[VMEM] * 9,
        out_specs=(VMEM, ANY, ANY, ANY, ANY, VMEM),
        scratch_shapes=[
            buffer((T, 768), BF16),
            buffer((T, 768), BF16),
            buffer((4, 8, T), F32),
            buffer((8, 768), F32),
            buffer((576, 768), BF16),
            buffer((384, 768), BF16),
            buffer((768, 768), BF16),
            buffer((768, 768), BF16),
            buffer((8, 8, 128), F32),
            buffer((8, 8, 128), F32),
            buffer((1024, 128), F32),
            buffer((2, T, 128), F32),
            buffer((1024, 768), BF16),
            buffer((1024, 768), BF16),
            buffer((1024, 768), BF16),
            buffer((1024, 768), BF16),
            buffer((6, 1024, HD), BF16),
            buffer((6, 1024, HD), BF16),
            buffer((6, 1024, HD), BF16),
            buffer((6, 1024, HD), BF16),
            buffer((6, 1024, HD), BF16),
            buffer((6, T, T), BF16),
            buffer((6, T, 2 * T), BF16),
            buffer((6, T, 3 * T), BF16),
            buffer((6, T, 4 * T), BF16),
            buffer((1024, 384), BF16),
            buffer((2, T, 768), F32),
            buffer((2, 1024, 768), BF16),
            buffer((2, 1024, 768), BF16),
            buffer((2, T, 768), BF16),
            buffer((2, T, 768), BF16),
            buffer((2, T, 768), F32),
            buffer((2, T, 768), BF16),
            buffer((2, T, 768), BF16),
            buffer((HD, 1024), F32),
            buffer((HD, 1024), F32),
            buffer((2, 384, 768), F32),
            buffer((768, 768), F32),
            buffer((3, 768, 768), BF16),
            buffer((3, 768, 768), BF16),
            buffer((3, 384, 768), BF16),
            buffer((3, 3, 96, 768), BF16),
            buffer((T, 768), BF16),
            buffer((T, 768), BF16),
            buffer((T, 768), BF16),
            buffer((1, 16, 768), F32),
            buffer((3, 16, 768), F32),
            buffer((8, 768), F32),
            buffer((7, 8, 768), F32),
            pltpu.SemaphoreType.DMA((copies,)),
            pltpu.SemaphoreType.DMA((copies,)),
            pltpu.SemaphoreType.DMA((5,)),
        ],
        compiler_params=pltpu.CompilerParams(
            collective_id=0, has_side_effects=True, vmem_limit_bytes=66500000
        ),
    )(
        tokens,
        cotangent,
        info,
        vectors,
        biases,
        qkv_rows,
        out_weight,
        fc_weight,
        proj_weight,
    )
    output, tokens_grad, dproj, dfc, dattn, small = outs

    def all_groups(value):
        if dp_size == GROUP:
            return value.astype(F32)
        sets = [[g * GROUP + i for g in range(dp_size // GROUP)] for i in range(GROUP)]
        return lax.psum(value.astype(F32), "dp", axis_index_groups=sets)

    dproj, dfc, dattn, small = map(all_groups, (dproj, dfc, dattn, small))
    dqkv_weight = jnp.transpose(dattn[:576].reshape(3, 192, 768), (2, 0, 1))
    return (
        output,
        tokens_grad,
        small[0],
        small[1],
        dqkv_weight,
        small[7, :576].reshape(3, 192),
        dattn[576:],
        small[4],
        small[2],
        small[3],
        dfc,
        small[6],
        dproj,
        small[5],
    )


def solution(mesh):
    row, flat = P("dp", "tp", None), P("dp", "tp")
    in_specs = (
        row,
        row,
        flat,
        flat,
        P("dp"),
        P(),
        P(),
        P(None, None, "tp"),
        P(None, "tp"),
        P("tp", None),
        P(),
        P(),
        P(),
        P(None, "tp"),
        P("tp"),
        P("tp", None),
        P(),
    )
    out_specs = (
        row,
        row,
        P(),
        P(),
        P(None, None, "tp"),
        P(None, "tp"),
        P("tp", None),
        P(),
        P(),
        P(),
        P(None, "tp"),
        P("tp"),
        P("tp", None),
        P(),
    )
    return jax.shard_map(
        functools.partial(local, mesh.shape["dp"]),
        mesh=mesh,
        in_specs=in_specs,
        out_specs=out_specs,
        check_vma=False,
    )
```

```python
import functools

import jax
import jax.numpy as jnp
from jax import lax
from jax.experimental import pallas as pl
from jax.experimental.pallas import tpu as pltpu
from jax.sharding import PartitionSpec as P

HD = 64
EPSILON = 1e-05
SCALE = HD ** (-0.5)
EXP2_SCALE = SCALE * 1.4426950408889634
GELU_A = 0.7978845608028654
GELU_B = 0.044715
T = 256
F32 = jnp.float32
BF16 = jnp.bfloat16
NN = (((1,), (0,)), ((), ()))
NT = (((1,), (1,)), ((), ()))
TN = (((0,), (0,)), ((), ()))
MESH = pl.DeviceIdType.MESH
GROUP = 8


def dot(a, b, dims=NN):
    return lax.dot_general(a, b, dims, preferred_element_type=F32)


def sub_rows(base, size, chunk, body):
    def step(i, carry):
        body(pl.ds(pl.multiple_of(base + i * chunk, chunk), chunk), i * chunk)
        return carry

    lax.fori_loop(0, size // chunk, step, 0)


class Links:
    def __init__(self, send_sems, recv_sems):
        self.send_sems, self.recv_sems = send_sems, recv_sems
        self.copies = []
        self.sent = []

    def send(self, source, target, device):
        index = len(self.copies)
        copy = pltpu.make_async_remote_copy(
            src_ref=source,
            dst_ref=target,
            send_sem=self.send_sems.at[index],
            recv_sem=self.recv_sems.at[index],
            device_id=device,
            device_id_type=MESH,
        )
        copy.start()
        self.copies.append(copy)
        return copy

    def wait_send(self, copy):
        copy.wait_send()
        self.sent.append(copy)

    def finish(self):
        for copy in self.copies:
            if not any(copy is other for other in self.sent):
                copy.wait_send()


def layer_kernel(
    dp_size,
    tok_ref,
    cot_ref,
    seg_ref,
    valid_ref,
    half_ref,
    gain1_ref,
    shift1_ref,
    qkv_bias_ref,
    out_bias_ref,
    gain2_ref,
    shift2_ref,
    fc_bias_ref,
    proj_bias_ref,
    wqkv_hbm,
    wout_hbm,
    wfc_hbm,
    wproj_hbm,
    out_ref,
    tgrad_ref,
    dproj_ref,
    dfc_ref,
    dattn_ref,
    small_ref,
    tok_own_ref,
    cot_own_ref,
    wqkv_ref,
    wfc_ref,
    wproj_ref,
    tok_in,
    cot_in,
    info_own,
    info_buf,
    bias_own,
    bias_in,
    wqkv_in,
    wout_all,
    wfc_in,
    wproj_in,
    count_out,
    count_in,
    seg_col,
    weight_col,
    normed,
    normed2,
    grad_full,
    attn_grad,
    q_s,
    k_s,
    v_s,
    o_s,
    do_s,
    p0,
    p1,
    p2,
    p3,
    att,
    middle,
    hid,
    dpre,
    give,
    got,
    own,
    give2,
    got2,
    key_acc,
    value_acc,
    proj_acc,
    proj_give,
    proj_got,
    proj_x_got,
    near_got,
    far_got,
    part,
    acc,
    x_give,
    x_got,
    y_got,
    out_own,
    out_give,
    tg_give,
    tg_got,
    small_a,
    small_sum,
    small_in,
    send_sems,
    recv_sems,
    local_sems,
):
    d = lax.axis_index("dp")
    t = lax.axis_index("tp")
    x = t // 2
    c = t - 2 * x
    t_core = t + 1 - 2 * c
    t_chip = lax.rem(t + 2, 4)
    t_both = 3 - t
    y = lax.rem(d, 2)
    group_first = d - lax.rem(d, GROUP)
    place = d - group_first
    z = place // 2
    d_y = d + 1 - 2 * y
    side_z = lax.rem(z, 2)
    far_z = z // 2
    d_near = d + 2 - 4 * side_z
    d_far = d + 4 - 8 * far_z
    fourth = 2 * y + side_z

    def d_flip(bit):
        size = 1 << bit
        return d + size - 2 * size * lax.rem(d // size, 2)

    dqkv = dpre
    count_bits = dp_size.bit_length() - 1
    links = Links(send_sems, recv_sems)
    send = links.send

    barrier = pltpu.get_barrier_semaphore()
    peers = [(d, t_core), (d, t_chip), (d, t_both)]
    peers += [(group_first + lax.rem(place + k, GROUP), t) for k in range(1, GROUP)]
    peers += [(d_flip(bit), t) for bit in range(3, count_bits)]
    for peer in peers:
        pl.semaphore_signal(barrier, inc=1, device_id=peer, device_id_type=MESH)
    loads = [
        pltpu.make_async_copy(source, target, local_sems.at[8 + index])
        for index, (source, target) in enumerate(
            (
                (tok_ref.at[x], tok_own_ref),
                (wqkv_hbm, wqkv_ref),
                (wout_hbm, wout_all.at[0:192]),
                (cot_ref.at[x], cot_own_ref),
                (wfc_hbm, wfc_ref),
                (wproj_hbm, wproj_ref),
            )
        )
    ]
    for load in loads:
        load.start()

    def block_rows(index):
        return pl.ds(pl.multiple_of(index * T, T), T)

    gain1, shift1, out_bias, gain2, shift2, proj_bias = (
        ref[...].reshape(1, 768)
        for ref in (gain1_ref, shift1_ref, out_bias_ref, gain2_ref, shift2_ref, proj_bias_ref)
    )

    for row in range(2):
        info_own[row, 0:1, :] = seg_ref[row : row + 1, :].astype(F32)
        info_own[row, 1:2, :] = valid_ref[row : row + 1, :].astype(F32)
        info_own[row, 2:3, :] = jnp.full((1, T), half_ref[row], jnp.int32).astype(F32)
        info_own[row, 3:8, :] = jnp.zeros((5, T), F32)
    bias_own[...] = jnp.zeros_like(bias_own)
    bias_own[0:1, :] = fc_bias_ref[...].reshape(1, 768)
    for piece in range(3):
        bias_own[1:2, piece * 192 : (piece + 1) * 192] = qkv_bias_ref[piece : piece + 1, :]
    info_buf[t] = info_own[x]
    for ref in (small_a, count_out):
        ref[...] = jnp.zeros_like(ref)

    pl.semaphore_wait(barrier, len(peers))
    info_copies = [
        send(info_own.at[x], info_buf.at[t], (d, t_core)),
        send(info_own.at[1 - x], info_buf.at[t], (d, t_chip)),
        send(info_own.at[1 - x], info_buf.at[t], (d, t_both)),
    ]
    bias_copy = send(bias_own, bias_in, (d, t_chip))
    tok_copy = send(tok_ref.at[1 - x], tok_in, (d, t_chip))

    class Fetch:
        def __init__(self, source, target, base, rows, first):
            self.source, self.target, self.base = source, target, base
            self.quarter, self.first, self.state = rows // 4, first, 0

        def view(self, ref, base, index, start, size):
            offset = pl.multiple_of(base + index * self.quarter + start, 16)
            return ref.at[pl.ds(offset, size)]

        def mine(self, index, start=0, size=None):
            return self.view(self.target, self.base, index, start, size or self.quarter)

        def start(self):
            here = self.view(self.source, 0, fourth, 0, self.quarter)
            self.copy = send(here, self.mine(fourth), (d, t_chip))

        def share(self):
            self.copy.wait_recv()
            here = self.mine(fourth)
            self.y_copy = send(here, here, (d_y, t))
            self.z_copy = send(here, here, (d_near, t))

        def cross(self):
            from_y = fourth + 2 - 4 * y
            from_z = fourth + 1 - 2 * side_z
            self.y_copy.wait_recv()
            here = self.mine(from_y, 0, self.first)
            self.last = [send(here, here, (d_near, t))]
            self.z_copy.wait_recv()
            here = self.mine(from_z, self.first, self.quarter - self.first)
            self.last.append(send(here, here, (d_y, t)))

        def finish(self):
            for copy in self.last:
                copy.wait_recv()

    fetch_qkv = Fetch(wqkv_hbm, wqkv_in, 0, 576, 80)
    fetch_out = Fetch(wout_hbm, wout_all, 192, 192, 32)
    fetch_fc = Fetch(wfc_hbm, wfc_in, 0, 768, 96)
    fetch_proj = Fetch(wproj_hbm, wproj_in, 0, 768, 96)
    fetch_qkv.start()
    fetch_out.start()

    def moments(values):
        average = jnp.mean(values, axis=-1, keepdims=True)
        centered = values - average
        spread = jnp.mean(centered * centered, axis=-1, keepdims=True)
        inverse = lax.rsqrt(spread + EPSILON)
        return centered * inverse, inverse

    def norm_one(load, index):
        base = index * T

        def body(rows, at):
            scaled, _ = moments(load(at))
            normed[rows, :] = (scaled * gain1 + shift1).astype(BF16)

        sub_rows(base, T, 64, body)

    def tok_own(at):
        return tok_own_ref[pl.ds(at, 64), :].astype(F32)

    def tok_other(at):
        return tok_in[pl.ds(at, 64), :].astype(F32)

    loads[0].wait()
    norm_one(tok_own, t)
    normed_copies = [send(normed.at[block_rows(t)], normed.at[block_rows(t)], (d, t_core))]
    tok_copy.wait_recv()
    fetch_fc.start()

    norm_one(tok_other, t_chip)
    normed_copies.append(
        send(normed.at[block_rows(t_chip)], normed.at[block_rows(t_chip)], (d, t_core))
    )
    for copy in info_copies:
        copy.wait_recv()

    half = info_buf[0, 2:3, 0:1]
    count = jnp.sum(info_buf[0, 1:2, :], axis=1, keepdims=True)
    for index in range(1, 4):
        count = count + jnp.sum(info_buf[index, 1:2, :], axis=1, keepdims=True)
    counts = [count * (1.0 - half), count * half]
    count_peers = [(d, t_chip)] + [(d_flip(bit), t) for bit in range(count_bits)]
    count_copies = []

    def count_start():
        step = len(count_copies)
        if step < len(count_peers):
            count_out[step, 0:1, :] = jnp.broadcast_to(counts[0], (1, 128))
            count_out[step, 1:2, :] = jnp.broadcast_to(counts[1], (1, 128))
            count_copies.append(send(count_out.at[step], count_in.at[step], count_peers[step]))

    def count_end():
        step = len(count_copies) - 1
        count_copies[step].wait_recv()
        counts[0] = counts[0] + count_in[step, 0:1, 0:1]
        counts[1] = counts[1] + count_in[step, 1:2, 0:1]

    count_start()
    seg_row = jnp.concatenate([info_buf[i, 0:1, :] for i in range(4)], axis=1)
    for index in range(4):
        row = jnp.broadcast_to(info_buf[index, 0:1, :], (128, T))
        seg_col[index * T : (index + 1) * T, :] = row.T
    for copy in normed_copies:
        copy.wait_recv()

    def project(side, weight):
        bias = (bias_own if side == 0 else bias_in)[1:2, 0:576]

        def body(rows, at):
            value = (dot(normed[rows, :], weight[...], NT) + bias).astype(BF16)
            for piece, ref in enumerate((q_s, k_s, v_s)):
                for h in range(3):
                    lane = piece * 192 + h * HD
                    ref[3 * side + h, rows, :] = value[:, lane : lane + HD]

        sub_rows(0, 4 * T, T, body)

    p_refs = (p0, p1, p2, p3)

    def attend(first):
        def head(h, carry):
            for index, p_ref in enumerate(p_refs):
                start, stop = index * T, (index + 1) * T
                rows = slice(start, stop)
                scores = dot(q_s[h, rows, :], k_s[h, 0:stop, :], NT) * EXP2_SCALE
                query_at = start + lax.broadcasted_iota(jnp.int32, (T, stop), 0)
                key_at = lax.broadcasted_iota(jnp.int32, (T, stop), 1)
                allowed = (key_at <= query_at) & (seg_col[rows, 0:1] == seg_row[:, 0:stop])
                scores = jnp.where(allowed, scores, -1e30)
                top = jnp.max(scores, axis=1, keepdims=True)
                exponent = jnp.exp2(scores - top)
                inverse = 1.0 / jnp.sum(exponent, axis=1, keepdims=True)
                low = (exponent * inverse).astype(BF16)
                p_ref[h] = low
                o_s[h, rows, :] = dot(low, v_s[h, 0:stop, :]).astype(BF16)
            return carry

        lax.fori_loop(first, first + 1, head, 0)

    loads[1].wait()
    project(0, wqkv_ref)
    fetch_qkv.share()
    fetch_proj.start()
    attend(0)
    fetch_out.share()
    cot_copy = send(cot_ref.at[1 - x], cot_in, (d, t_chip))
    attend(1)
    count_end()
    count_start()
    fetch_fc.share()
    attend(2)
    fetch_qkv.cross()
    fetch_out.cross()
    bias_copy.wait_recv()
    fetch_qkv.finish()
    project(1, wqkv_in)
    count_end()
    count_start()
    attend(3)
    fetch_proj.share()
    attend(4)
    attend(5)
    fetch_fc.cross()
    count_end()
    count_start()
    for h in range(6):
        att[:, h * HD : (h + 1) * HD] = o_s[h]

    def scatter(partial, give_ref, got_ref, before=()):
        for copy in before:
            links.wait_send(copy)
        copies = []
        for slot, index in enumerate((t_core, t_both)):
            give_ref[slot] = partial(index).astype(BF16)
            copies.append(send(give_ref.at[slot], got_ref.at[slot], (d, t_core)))
        for slot, index in enumerate((t, t_chip)):
            own[slot] = partial(index)
        return copies

    def out_partial(index):
        return dot(att[block_rows(index), :], wout_all[...])

    fetch_out.finish()
    loads[2].wait()
    attn_copies = scatter(out_partial, give, got)

    normed2_copies = []
    for slot, index in enumerate((t, t_chip)):
        attn_copies[slot].wait_recv()
        load = tok_own if slot == 0 else tok_other

        def body(rows, at, slot=slot, index=index, load=load):
            value = load(at) + own[slot, rows, :] + got[slot, rows, :].astype(F32) + out_bias
            middle[slot, rows, :] = value
            scaled, _ = moments(value)
            normed2[pl.ds(pl.multiple_of(index * T + at, 64), 64), :] = (
                scaled * gain2 + shift2
            ).astype(BF16)

        sub_rows(0, T, 64, body)
        rows = block_rows(index)
        normed2_copies.append(send(normed2.at[rows], normed2.at[rows], (d, t_core)))
    while len(count_copies) < len(count_peers):
        count_end()
        count_start()
    count_end()

    row_scale = (counts[0] + counts[1]) / (2.0 * jnp.where(half == 0.0, counts[0], counts[1]))
    cot_copy.wait_recv()
    for load in loads[3:]:
        load.wait()
    grad_copies = []
    for slot, index in enumerate((t, t_chip)):
        row = jnp.broadcast_to(info_buf[index, 1:2, :] * row_scale, (128, T))
        weight_col[slot] = row.T

    def out_grad(slot, rows, at):
        source = cot_own_ref[rows, :] if slot == 0 else cot_in[rows, :]
        return source.astype(F32) * weight_col[slot, rows, 0:1]

    for slot, index in enumerate((t, t_chip)):

        def body(rows, at, slot=slot, index=index):
            low = out_grad(slot, rows, at).astype(BF16)
            grad_full[pl.ds(pl.multiple_of(index * T + at, 64), 64), :] = low
            small_a[0, 5:6, :] += jnp.sum(low.astype(F32), axis=0, keepdims=True)

        sub_rows(0, T, 64, body)
        rows = block_rows(index)
        grad_copies.append(send(grad_full.at[rows], grad_full.at[rows], (d, t_core)))
    for copy in normed2_copies + grad_copies:
        copy.wait_recv()

    def mlp(side, fc, proj):
        bias = (bias_own if side == 0 else bias_in)[0:1, :]

        def body(rows, at):
            pre = dot(normed2[rows, :], fc[...]) + bias
            square = pre * pre
            bent = jnp.tanh(GELU_A * (pre + GELU_B * square * pre))
            rise = 0.5 * (1.0 + bent)
            hid[side, rows, :] = (pre * rise).astype(BF16)
            slope = rise + 0.5 * pre * (1.0 - bent * bent) * (
                GELU_A + (3.0 * GELU_A * GELU_B) * square
            )
            low = (dot(grad_full[rows, :], proj[...], NT) * slope).astype(BF16)
            dpre[side, rows, :] = low
            small_a[0, 6 + 2 * side : 7 + 2 * side, :] += jnp.sum(
                low.astype(F32), axis=0, keepdims=True
            )

        sub_rows(0, 4 * T, T, body)

    def proj_product(side, rows):
        return dot(hid[side, :, rows], grad_full[...], TN)

    def half_rows(index):
        return pl.ds(pl.multiple_of(index * 384, 384), 384)

    fetch_proj.cross()
    mlp(0, wfc_ref, wproj_ref)
    proj_give[0] = proj_product(0, half_rows(1 - y)).astype(BF16)
    proj_y = [send(proj_give.at[0], proj_got.at[0], (d_y, t))]
    fetch_fc.finish()
    fetch_proj.finish()
    mlp(1, wfc_in, wproj_in)
    proj_give[1] = proj_product(1, half_rows(1 - y)).astype(BF16)
    proj_y.append(send(proj_give.at[1], proj_got.at[1], (d_y, t)))

    def fc_product(side, chunk):
        return dot(normed2[:, chunk * 384 : (chunk + 1) * 384], dpre[side], TN)

    class Chunk:
        def __init__(self, slot, out, base, y_step, acc_ref, low, raw):
            self.out, self.base = out, base + y * y_step
            self.acc, self.low, self.raw = acc_ref, low, raw
            self.near_got, self.far_got = near_got.at[slot], far_got.at[slot]
            self.sem = local_sems.at[slot]
            self.half, self.fin = 96 * side_z, 96 * side_z + 48 * far_z

        def rows(self, start, size):
            return pl.ds(pl.multiple_of(start, 16), size)

        def total(self, rows):
            value = self.acc[rows, :]
            return value + self.low[rows, :].astype(F32) if self.raw else value

        def near_start(self):
            if self.raw:
                self.y_copy.wait_recv()
            rows = self.rows(96 - self.half, 96)
            self.low[rows, :] = self.total(rows).astype(BF16)
            self.near_copy = send(self.low.at[rows], self.near_got, (d_near, t))

        def far_start(self):
            self.near_copy.wait_recv()
            inner = self.rows(48 - 48 * far_z, 48)
            rows = self.rows(self.half + 48 - 48 * far_z, 48)
            value = self.total(rows) + self.near_got[inner, :].astype(F32)
            self.low[rows, :] = value.astype(BF16)
            self.far_copy = send(self.low.at[rows], self.far_got, (d_far, t))

        def placed(self, start, size):
            return self.out.at[self.rows(self.base + start, size)]

        def far_back(self):
            inner = self.rows(48 * far_z, 48)
            rows = self.rows(self.fin, 48)
            value = self.total(rows) + self.near_got[inner, :].astype(F32)
            self.far_copy.wait_recv()
            value = value + self.far_got[...].astype(F32)
            self.low[rows, :] = value.astype(BF16)
            here, there = self.low.at[rows], self.placed(self.fin, 48)
            self.keep = pltpu.make_async_copy(here, there, self.sem)
            self.keep.start()
            self.copy = send(here, there, (d_far, t))

        def near_back(self):
            self.keep.wait()
            self.copy.wait_recv()
            there = self.placed(self.half, 96)
            self.copy = send(there, there, (d_near, t))

        def y_back(self):
            self.copy.wait_recv()
            there = self.placed(0, 192)
            self.copy = send(there, there, (d_y, t))

        def finish(self):
            self.copy.wait_recv()

    class Flow(Chunk):
        def __init__(self, slot, out, chunk):
            super().__init__(slot, out, chunk * 384, 192, acc.at[slot], y_got.at[slot], True)
            self.slot = slot
            self.x_copies = []

        def x_send(self, first=0, size=384):
            rows = slice(first, first + size)
            self.x_copies.append(
                send(x_give.at[self.slot, rows], x_got.at[self.slot, rows], (d, t_chip))
            )

        def y_start(self, fill):
            fill()
            for copy in self.x_copies:
                copy.wait_recv()
            slot = self.slot
            part[...] = part[...] + x_got[slot].astype(F32)
            other = pl.ds(pl.multiple_of((1 - y) * 192, 16), 192)
            mine = pl.ds(pl.multiple_of(y * 192, 16), 192)
            x_got[slot, other, :] = part[other, :].astype(BF16)
            self.y_copy = send(x_got.at[slot, other], y_got.at[slot], (d_y, t))
            acc[slot] = part[mine, :]

    fc_flows = [Flow(0, dfc_ref, 0), Flow(1, dfc_ref, 1)]
    attn_flows = [Flow(2, dattn_ref, 0), Flow(3, dattn_ref, 1)]
    proj_flows = []
    for chunk in range(2):
        rows = pl.ds(chunk * 192, 192)
        low = proj_got.at[0, rows]
        proj_flows.append(
            Chunk(4 + chunk, dproj_ref, chunk * 192, 384, proj_acc.at[rows], low, False)
        )

    def fc_fill(chunk):
        def fill():
            part[...] = fc_product(0, chunk)

        return fill

    for chunk in range(2):
        x_give[chunk] = fc_product(1, chunk).astype(BF16)
        fc_flows[chunk].x_send()

    def mlp_partial(index):
        rows = block_rows(index)
        return dot(hid[0, rows, :], wproj_ref[...]) + dot(hid[1, rows, :], wproj_in[...])

    mlp_copies = scatter(mlp_partial, give2, got2)
    for slot in range(2):
        mlp_copies[slot].wait_recv()

        def body(rows, at, slot=slot):
            value = (
                middle[slot, rows, :]
                + own[slot, rows, :]
                + got2[slot, rows, :].astype(F32)
                + proj_bias
            )
            (out_own, out_give)[slot][rows, :] = value.astype(BF16)

        sub_rows(0, T, 64, body)
    out_keep = pltpu.make_async_copy(out_own, out_ref.at[x], local_sems.at[7])
    out_keep.start()

    def norm2_partial(index):
        rows = block_rows(index)
        return dot(dpre[0, rows, :], wfc_ref[...], NT) + dot(dpre[1, rows, :], wfc_in[...], NT)

    back_copies = scatter(norm2_partial, give, got, attn_copies)
    def norm_back(upstream, values, gain):
        scaled, inverse = moments(values)
        pushed = upstream * gain
        mean_one = jnp.mean(pushed, axis=-1, keepdims=True)
        mean_two = jnp.mean(pushed * scaled, axis=-1, keepdims=True)
        gain_grad = jnp.sum(upstream * scaled, axis=0, keepdims=True)
        shift_grad = jnp.sum(upstream, axis=0, keepdims=True)
        return inverse * (pushed - mean_one - scaled * mean_two), gain_grad, shift_grad

    grad_copies = []
    for slot, index in enumerate((t, t_chip)):
        back_copies[slot].wait_recv()

        def body(rows, at, slot=slot, index=index):
            upstream = own[slot, rows, :] + got[slot, rows, :].astype(F32)
            part, gain_grad, shift_grad = norm_back(upstream, middle[slot, rows, :], gain2)
            value = out_grad(slot, rows, at) + part
            middle[slot, rows, :] = value
            low = value.astype(BF16)
            attn_grad[pl.ds(pl.multiple_of(index * T + at, 64), 64), :] = low
            small_a[0, 2:3, :] += gain_grad
            small_a[0, 3:4, :] += shift_grad
            small_a[0, 4:5, :] += jnp.sum(low.astype(F32), axis=0, keepdims=True)

        sub_rows(0, T, 64, body)
        rows = block_rows(index)
        grad_copies.append(send(attn_grad.at[rows], attn_grad.at[rows], (d, t_core)))
    for copy in grad_copies:
        copy.wait_recv()

    def spread_heads(rows, at):
        value = dot(attn_grad[rows, :], wout_all[...], NT)
        for h in range(6):
            do_s[h, rows, :] = value[:, h * HD : (h + 1) * HD].astype(BF16)

    sub_rows(0, 4 * T, T, spread_heads)
    x_give[3, 192:384, :] = dot(att[:, 192:384], attn_grad[...], TN).astype(BF16)

    def attend_back(first):
        def head(h, carry):
            query_t = q_s[h].T
            for index, p_ref in enumerate(p_refs):
                start, stop = index * T, (index + 1) * T
                rows = slice(start, stop)
                weights = p_ref[h]
                upstream = do_s[h, rows, :]
                row_dot = jnp.sum(
                    upstream.astype(F32) * o_s[h, rows, :].astype(F32), axis=1, keepdims=True
                )
                weight_grad = dot(upstream, v_s[h, 0:stop, :], NT)
                score_grad = (weights.astype(F32) * (weight_grad - row_dot)).astype(BF16)
                q_s[h, rows, :] = (dot(score_grad, k_s[h, 0:stop, :]) * SCALE).astype(BF16)
                key_part = dot(query_t[:, rows], score_grad)
                value_part = dot(upstream.T, weights)
                if start:
                    key_acc[:, 0:start] += key_part[:, 0:start]
                    value_acc[:, 0:start] += value_part[:, 0:start]
                key_acc[:, rows] = key_part[:, start:]
                value_acc[:, rows] = value_part[:, start:]
            k_s[h] = (key_acc[...] * SCALE).T.astype(BF16)
            v_s[h] = value_acc[...].T.astype(BF16)
            return carry

        lax.fori_loop(first, first + 1, head, 0)

    def dqkv_rows(side, first, last):
        return dqkv[side, :, first:last]

    def collect(side):
        for piece, ref in enumerate((q_s, k_s, v_s)):
            for h in range(3):
                lane = piece * 192 + h * HD
                dqkv[side, :, lane : lane + HD] = ref[3 * side + h]
        small_a[0, 7 + 2 * side : 8 + 2 * side, 0:576] = jnp.sum(
            dqkv[side, :, 0:576].astype(F32), axis=0, keepdims=True
        )

    attend_back(3)
    attend_back(4)
    attend_back(5)
    collect(1)
    x_give[3, 0:192, :] = dot(dqkv_rows(1, 384, 576), normed[...], TN).astype(BF16)
    attn_flows[1].x_send()
    x_give[2] = dot(dqkv_rows(1, 0, 384), normed[...], TN).astype(BF16)
    attn_flows[0].x_send()
    proj_y[1].wait_recv()
    mine = proj_product(1, half_rows(y)) + proj_got[1].astype(F32)
    proj_got[1] = mine.astype(BF16)
    proj_x = send(proj_got.at[1], proj_x_got, (d, t_chip))
    fc_flows[0].y_start(fc_fill(0))
    attend_back(0)
    fc_flows[1].y_start(fc_fill(1))
    proj_y[0].wait_recv()
    proj_acc[...] = proj_product(0, half_rows(y)) + proj_got[0].astype(F32)
    attend_back(1)
    fc_a, fc_b = fc_flows
    attn_a, attn_b = attn_flows
    proj_a, proj_b = proj_flows
    fc_a.near_start()
    attend_back(2)
    fc_a.far_start()
    fc_b.near_start()
    collect(0)

    def norm1_partial(index):
        rows = block_rows(index)
        return dot(dqkv[0, rows, 0:576], wqkv_ref[...]) + dot(dqkv[1, rows, 0:576], wqkv_in[...])

    back_copies = scatter(norm1_partial, give, got, back_copies)
    fc_a.far_back()
    fc_b.far_start()
    for slot in (1, 0):
        back_copies[slot].wait_recv()
        load = tok_own if slot == 0 else tok_other

        def body(rows, at, slot=slot, load=load):
            upstream = own[slot, rows, :] + got[slot, rows, :].astype(F32)
            part, gain_grad, shift_grad = norm_back(upstream, load(at), gain1)
            value = middle[slot, rows, :] + part
            if slot == 0:
                own[0, rows, :] = value
            else:
                tg_give[rows, :] = value.astype(BF16)
            small_a[0, 0:1, :] += gain_grad
            small_a[0, 1:2, :] += shift_grad

        sub_rows(0, T, 64, body)
        if slot == 1:
            tg_copy = send(tg_give, tg_got, (d, t_chip))
    tg_keep = [pltpu.make_async_copy(own.at[0], tgrad_ref.at[x], local_sems.at[14])]
    tg_keep[0].start()

    small_peers = [(d_y, t), (d_near, t), (d_far, t), (d, t_core), (d, t_chip)]
    small_copies = []

    def small_next():
        step = len(small_copies)
        if step == 0:
            small_sum[0] = small_a[0]
        else:
            small_copies[-1].wait_recv()
            rows = 16 if step < 4 else 6
            small_sum[step] = small_sum[step - 1]
            small_sum[step, 0:rows, :] += small_in[step - 1, 0:rows, :]
        small_copies.append(send(small_sum.at[step], small_in.at[step], small_peers[step]))

    small_next()

    def attn_fill(chunk):
        def fill():
            if chunk == 0:
                part[...] = dot(dqkv_rows(0, 0, 384), normed[...], TN)
            else:
                part[0:192, :] = dot(dqkv_rows(0, 384, 576), normed[...], TN)
                part[192:384, :] = dot(att[:, 0:192], attn_grad[...], TN)

        return fill

    attn_b.y_start(attn_fill(1))
    fc_a.near_back()
    fc_b.far_back()
    attn_b.near_start()
    small_next()
    fc_b.near_back()
    attn_a.y_start(attn_fill(0))
    fc_a.y_back()
    attn_b.far_start()
    fc_b.y_back()
    small_next()
    attn_b.far_back()
    attn_a.near_start()
    proj_x.wait_recv()
    proj_acc[...] += proj_x_got[...].astype(F32)
    proj_a.near_start()
    proj_b.near_start()
    small_next()
    out_copy = send(out_give, out_ref.at[x], (d, t_chip))
    attn_b.near_back()
    attn_a.far_start()
    small_next()
    attn_a.far_back()
    proj_a.far_start()
    proj_b.far_start()
    attn_b.y_back()
    proj_a.far_back()
    attn_a.near_back()
    proj_b.far_back()
    proj_a.near_back()
    attn_a.y_back()
    proj_b.near_back()
    proj_a.y_back()
    small_copies[4].wait_recv()
    small_ref[0:6, :] = small_sum[4, 0:6, :] + small_in[4, 0:6, :]
    small_ref[6:8, :] = small_sum[4, 6:8, :] + small_in[4, 8:10, :]
    proj_b.y_back()
    tg_copy.wait_recv()
    own[1] = tg_got[...].astype(F32)
    tg_keep.append(pltpu.make_async_copy(own.at[1], tgrad_ref.at[1 - x], local_sems.at[6]))
    tg_keep[1].start()
    out_copy.wait_recv()
    out_keep.wait()
    for flow in fc_flows + attn_flows + proj_flows:
        flow.finish()
    for copy in tg_keep:
        copy.wait()
    links.finish()


def finish_kernel(
    out_in, tgrad_in, dproj_in, dfc_in, dattn_in, small_in, out, tgrad, dproj, dfc, dqkv, dout, *small
):
    step = pl.program_id(0)
    out[...] = out_in[...]
    tgrad[...] = tgrad_in[...]
    dproj[...] = dproj_in[...].astype(F32)
    dfc[...] = dfc_in[...].astype(F32)

    @pl.when(step < 3)
    def _():
        dqkv[...] = dattn_in[...].astype(F32)

    @pl.when(step == 3)
    def _():
        dout[...] = dattn_in[...].astype(F32)
        for row, ref in enumerate(small[:7]):
            ref[...] = small_in[row, :]
        for piece in range(3):
            small[7][piece : piece + 1, :] = small_in[7:8, piece * 192 : (piece + 1) * 192]


def finish(output, tokens_grad, dproj, dfc, dattn, small):
    def rows(size, index):
        return pl.BlockSpec((size, 768), index)

    def same(i):
        return (i, 0)

    vector = jax.ShapeDtypeStruct((768,), F32)
    weight = jax.ShapeDtypeStruct((768, 768), F32)
    whole = pl.BlockSpec((768,), lambda i: (0,))
    return pl.pallas_call(
        finish_kernel,
        grid=(4,),
        out_shape=(
            jax.ShapeDtypeStruct((2 * T, 768), BF16),
            jax.ShapeDtypeStruct((2 * T, 768), F32),
            weight,
            weight,
            jax.ShapeDtypeStruct((576, 768), F32),
            jax.ShapeDtypeStruct((192, 768), F32),
        )
        + (vector,) * 7
        + (jax.ShapeDtypeStruct((3, 192), F32),),
        in_specs=[rows(128, same)] * 2
        + [rows(192, same)] * 3
        + [pl.BlockSpec((8, 768), lambda i: (0, 0))],
        out_specs=[rows(128, same)] * 2
        + [rows(192, same)] * 2
        + [rows(192, lambda i: (jnp.minimum(i, 2), 0)), rows(192, lambda i: (0, 0))]
        + [whole] * 7
        + [pl.BlockSpec((3, 192), lambda i: (0, 0))],
    )(output.reshape(2 * T, 768), tokens_grad.reshape(2 * T, 768), dproj, dfc, dattn, small)


VMEM = pl.BlockSpec(memory_space=pltpu.VMEM)
ANY = pl.BlockSpec(memory_space=pl.ANY)
SMEM = pl.BlockSpec(memory_space=pltpu.SMEM)


def local(
    dp_size,
    tokens,
    cotangent,
    segment_ids,
    valid_mask,
    row_half,
    norm1_gain,
    norm1_shift,
    qkv_weight,
    qkv_bias,
    out_weight,
    out_bias,
    norm2_gain,
    norm2_shift,
    fc_weight,
    fc_bias,
    proj_weight,
    proj_bias,
):
    qkv_rows = jnp.transpose(qkv_weight, (1, 2, 0)).reshape(576, 768)

    copies = 160

    def buffer(shape, dtype):
        return pltpu.VMEM(shape, dtype)

    outs = pl.pallas_call(
        functools.partial(layer_kernel, dp_size),
        out_shape=(
            jax.ShapeDtypeStruct((2, T, 768), BF16),
            jax.ShapeDtypeStruct((2, T, 768), F32),
            jax.ShapeDtypeStruct((768, 768), BF16),
            jax.ShapeDtypeStruct((768, 768), BF16),
            jax.ShapeDtypeStruct((768, 768), BF16),
            jax.ShapeDtypeStruct((8, 768), F32),
        ),
        in_specs=[ANY] * 2 + [VMEM] * 2 + [SMEM] + [VMEM] * 8 + [ANY] * 4,
        out_specs=(ANY, ANY, ANY, ANY, ANY, VMEM),
        scratch_shapes=[
            buffer((T, 768), BF16),
            buffer((T, 768), BF16),
            buffer((576, 768), BF16),
            buffer((768, 768), BF16),
            buffer((768, 768), BF16),
            buffer((T, 768), BF16),
            buffer((T, 768), BF16),
            buffer((2, 8, T), F32),
            buffer((4, 8, T), F32),
            buffer((8, 768), F32),
            buffer((8, 768), F32),
            buffer((576, 768), BF16),
            buffer((384, 768), BF16),
            buffer((768, 768), BF16),
            buffer((768, 768), BF16),
            buffer((8, 8, 128), F32),
            buffer((8, 8, 128), F32),
            buffer((1024, 128), F32),
            buffer((2, T, 128), F32),
            buffer((1024, 768), BF16),
            buffer((1024, 768), BF16),
            buffer((1024, 768), BF16),
            buffer((1024, 768), BF16),
            buffer((6, 1024, HD), BF16),
            buffer((6, 1024, HD), BF16),
            buffer((6, 1024, HD), BF16),
            buffer((6, 1024, HD), BF16),
            buffer((6, 1024, HD), BF16),
            buffer((6, T, T), BF16),
            buffer((6, T, 2 * T), BF16),
            buffer((6, T, 3 * T), BF16),
            buffer((6, T, 4 * T), BF16),
            buffer((1024, 384), BF16),
            buffer((2, T, 768), F32),
            buffer((2, 1024, 768), BF16),
            buffer((2, 1024, 768), BF16),
            buffer((2, T, 768), BF16),
            buffer((2, T, 768), BF16),
            buffer((2, T, 768), F32),
            buffer((2, T, 768), BF16),
            buffer((2, T, 768), BF16),
            buffer((HD, 1024), F32),
            buffer((HD, 1024), F32),
            buffer((384, 768), F32),
            buffer((2, 384, 768), BF16),
            buffer((2, 384, 768), BF16),
            buffer((384, 768), BF16),
            buffer((6, 96, 768), BF16),
            buffer((6, 48, 768), BF16),
            buffer((384, 768), F32),
            buffer((4, 192, 768), F32),
            buffer((4, 384, 768), BF16),
            buffer((4, 384, 768), BF16),
            buffer((4, 192, 768), BF16),
            buffer((T, 768), BF16),
            buffer((T, 768), BF16),
            buffer((T, 768), BF16),
            buffer((T, 768), BF16),
            buffer((1, 16, 768), F32),
            buffer((5, 16, 768), F32),
            buffer((5, 16, 768), F32),
            pltpu.SemaphoreType.DMA((copies,)),
            pltpu.SemaphoreType.DMA((copies,)),
            pltpu.SemaphoreType.DMA((15,)),
        ],
        compiler_params=pltpu.CompilerParams(
            collective_id=0, has_side_effects=True, vmem_limit_bytes=66500000
        ),
    )(
        tokens,
        cotangent,
        segment_ids,
        valid_mask,
        row_half,
        norm1_gain,
        norm1_shift,
        qkv_bias,
        out_bias,
        norm2_gain,
        norm2_shift,
        fc_bias,
        proj_bias,
        qkv_rows,
        out_weight,
        fc_weight,
        proj_weight,
    )
    output, tokens_grad, dproj, dfc, dattn, small = outs

    def all_groups(value):
        if dp_size == GROUP:
            return value
        sets = [[g * GROUP + i for g in range(dp_size // GROUP)] for i in range(GROUP)]
        return lax.psum(value.astype(F32), "dp", axis_index_groups=sets)

    dproj, dfc, dattn, small = map(all_groups, (dproj, dfc, dattn, small))
    outs = finish(output, tokens_grad, dproj, dfc, dattn, small)
    output, tokens_grad, dproj, dfc, dqkv, dout = outs[:6]
    gain1, shift1, gain2, shift2, dout_bias, dproj_bias, dfc_bias, dqkv_bias = outs[6:]
    return (
        output.reshape(2, T, 768),
        tokens_grad.reshape(2, T, 768),
        gain1,
        shift1,
        jnp.transpose(dqkv.reshape(3, 192, 768), (2, 0, 1)),
        dqkv_bias,
        dout,
        dout_bias,
        gain2,
        shift2,
        dfc,
        dfc_bias,
        dproj,
        dproj_bias,
    )


def solution(mesh):
    row, flat = P("dp", "tp", None), P("dp", "tp")
    in_specs = (
        row,
        row,
        flat,
        flat,
        P("dp"),
        P(),
        P(),
        P(None, None, "tp"),
        P(None, "tp"),
        P("tp", None),
        P(),
        P(),
        P(),
        P(None, "tp"),
        P("tp"),
        P("tp", None),
        P(),
    )
    out_specs = (
        row,
        row,
        P(),
        P(),
        P(None, None, "tp"),
        P(None, "tp"),
        P("tp", None),
        P(),
        P(),
        P(),
        P(None, "tp"),
        P("tp"),
        P("tp", None),
        P(),
    )
    return jax.shard_map(
        functools.partial(local, mesh.shape["dp"]),
        mesh=mesh,
        in_specs=in_specs,
        out_specs=out_specs,
        check_vma=False,
    )
```

```python
import functools

import jax
import jax.numpy as jnp
from jax import lax
from jax.experimental import pallas as pl
from jax.experimental.pallas import tpu as pltpu
from jax.sharding import PartitionSpec as P

HD = 64
EPSILON = 1e-05
SCALE = HD ** (-0.5)
EXP2_SCALE = SCALE * 1.4426950408889634
GELU_A = 0.7978845608028654
GELU_B = 0.044715
T = 256
F32 = jnp.float32
BF16 = jnp.bfloat16
NN = (((1,), (0,)), ((), ()))
NT = (((1,), (1,)), ((), ()))
TN = (((0,), (0,)), ((), ()))
MESH = pl.DeviceIdType.MESH
GROUP = 8


def dot(a, b, dims=NN):
    return lax.dot_general(a, b, dims, preferred_element_type=F32)


def sub_rows(base, size, chunk, body):
    def step(i, carry):
        body(pl.ds(pl.multiple_of(base + i * chunk, chunk), chunk), i * chunk)
        return carry

    lax.fori_loop(0, size // chunk, step, 0)


class Links:
    def __init__(self, send_sems, recv_sems):
        self.send_sems, self.recv_sems = send_sems, recv_sems
        self.copies = []
        self.sent = []

    def send(self, source, target, device):
        index = len(self.copies)
        copy = pltpu.make_async_remote_copy(
            src_ref=source,
            dst_ref=target,
            send_sem=self.send_sems.at[index],
            recv_sem=self.recv_sems.at[index],
            device_id=device,
            device_id_type=MESH,
        )
        copy.start()
        self.copies.append(copy)
        return copy

    def wait_send(self, copy):
        copy.wait_send()
        self.sent.append(copy)

    def finish(self):
        for copy in self.copies:
            if not any(copy is other for other in self.sent):
                copy.wait_send()


def layer_kernel(
    dp_size,
    tok_ref,
    cot_ref,
    seg_ref,
    valid_ref,
    half_ref,
    gain1_ref,
    shift1_ref,
    qkv_bias_ref,
    out_bias_ref,
    gain2_ref,
    shift2_ref,
    fc_bias_ref,
    proj_bias_ref,
    wqkv_hbm,
    wout_hbm,
    wfc_hbm,
    wproj_hbm,
    out_ref,
    tgrad_ref,
    dproj_ref,
    dfc_ref,
    dattn_ref,
    small_ref,
    tok_own_ref,
    cot_own_ref,
    wqkv_ref,
    wfc_ref,
    wproj_ref,
    tok_in,
    cot_in,
    info_own,
    info_buf,
    bias_own,
    bias_in,
    wqkv_in,
    wout_all,
    wfc_in,
    wproj_in,
    count_out,
    count_in,
    seg_col,
    weight_col,
    normed,
    normed2,
    grad_full,
    attn_grad,
    q_s,
    k_s,
    v_s,
    o_s,
    do_s,
    p0,
    p1,
    p2,
    p3,
    att,
    middle,
    hid,
    dpre,
    give,
    got,
    own,
    give2,
    got2,
    key_acc,
    value_acc,
    proj_acc,
    proj_give,
    proj_got,
    proj_x_got,
    near_got,
    far_got,
    part,
    acc,
    x_give,
    x_got,
    y_got,
    out_own,
    out_give,
    tg_give,
    tg_got,
    small_a,
    small_sum,
    small_in,
    send_sems,
    recv_sems,
    local_sems,
):
    d = lax.axis_index("dp")
    t = lax.axis_index("tp")
    x = t // 2
    c = t - 2 * x
    t_core = t + 1 - 2 * c
    t_chip = lax.rem(t + 2, 4)
    t_both = 3 - t
    y = lax.rem(d, 2)
    group_first = d - lax.rem(d, GROUP)
    place = d - group_first
    z = place // 2
    d_y = d + 1 - 2 * y
    side_z = lax.rem(z, 2)
    far_z = z // 2
    d_near = d + 2 - 4 * side_z
    d_far = d + 4 - 8 * far_z
    fourth = 2 * y + side_z

    def d_flip(bit):
        size = 1 << bit
        return d + size - 2 * size * lax.rem(d // size, 2)

    dqkv = dpre
    count_bits = dp_size.bit_length() - 1
    links = Links(send_sems, recv_sems)
    send = links.send

    barrier = pltpu.get_barrier_semaphore()
    peers = [(d, t_core), (d, t_chip), (d, t_both)]
    peers += [(group_first + lax.rem(place + k, GROUP), t) for k in range(1, GROUP)]
    peers += [(d_flip(bit), t) for bit in range(3, count_bits)]
    for peer in peers:
        pl.semaphore_signal(barrier, inc=1, device_id=peer, device_id_type=MESH)
    loads = [
        pltpu.make_async_copy(source, target, local_sems.at[8 + index])
        for index, (source, target) in enumerate(
            (
                (tok_ref.at[x], tok_own_ref),
                (wqkv_hbm, wqkv_ref),
                (wout_hbm, wout_all.at[0:192]),
                (cot_ref.at[x], cot_own_ref),
                (wfc_hbm, wfc_ref),
                (wproj_hbm, wproj_ref),
            )
        )
    ]
    for load in loads:
        load.start()

    def block_rows(index):
        return pl.ds(pl.multiple_of(index * T, T), T)

    gain1, shift1, out_bias, gain2, shift2, proj_bias = (
        ref[...].reshape(1, 768)
        for ref in (gain1_ref, shift1_ref, out_bias_ref, gain2_ref, shift2_ref, proj_bias_ref)
    )

    for row in range(2):
        info_own[row, 0:1, :] = seg_ref[row : row + 1, :].astype(F32)
        info_own[row, 1:2, :] = valid_ref[row : row + 1, :].astype(F32)
        info_own[row, 2:3, :] = jnp.full((1, T), half_ref[row], jnp.int32).astype(F32)
        info_own[row, 3:8, :] = jnp.zeros((5, T), F32)
    bias_own[...] = jnp.zeros_like(bias_own)
    bias_own[0:1, :] = fc_bias_ref[...].reshape(1, 768)
    for piece in range(3):
        bias_own[1:2, piece * 192 : (piece + 1) * 192] = qkv_bias_ref[piece : piece + 1, :]
    info_buf[t] = info_own[x]
    for ref in (small_a, count_out):
        ref[...] = jnp.zeros_like(ref)

    pl.semaphore_wait(barrier, len(peers))
    info_copies = [
        send(info_own.at[x], info_buf.at[t], (d, t_core)),
        send(info_own.at[1 - x], info_buf.at[t], (d, t_chip)),
        send(info_own.at[1 - x], info_buf.at[t], (d, t_both)),
    ]
    bias_copy = send(bias_own, bias_in, (d, t_chip))
    tok_copy = send(tok_ref.at[1 - x], tok_in, (d, t_chip))

    class Fetch:
        def __init__(self, source, target, base, rows, first):
            self.source, self.target, self.base = source, target, base
            self.quarter, self.first, self.state = rows // 4, first, 0

        def view(self, ref, base, index, start, size):
            offset = pl.multiple_of(base + index * self.quarter + start, 16)
            return ref.at[pl.ds(offset, size)]

        def mine(self, index, start=0, size=None):
            return self.view(self.target, self.base, index, start, size or self.quarter)

        def start(self):
            here = self.view(self.source, 0, fourth, 0, self.quarter)
            self.copy = send(here, self.mine(fourth), (d, t_chip))

        def share(self):
            self.copy.wait_recv()
            here = self.mine(fourth)
            self.y_copy = send(here, here, (d_y, t))
            self.z_copy = send(here, here, (d_near, t))

        def cross(self):
            from_y = fourth + 2 - 4 * y
            from_z = fourth + 1 - 2 * side_z
            self.y_copy.wait_recv()
            here = self.mine(from_y, 0, self.first)
            self.last = [send(here, here, (d_near, t))]
            self.z_copy.wait_recv()
            here = self.mine(from_z, self.first, self.quarter - self.first)
            self.last.append(send(here, here, (d_y, t)))

        def finish(self):
            for copy in self.last:
                copy.wait_recv()

    fetch_qkv = Fetch(wqkv_hbm, wqkv_in, 0, 576, 80)
    fetch_out = Fetch(wout_hbm, wout_all, 192, 192, 32)
    fetch_fc = Fetch(wfc_hbm, wfc_in, 0, 768, 96)
    fetch_proj = Fetch(wproj_hbm, wproj_in, 0, 768, 96)
    fetch_qkv.start()
    fetch_out.start()

    def moments(values):
        average = jnp.mean(values, axis=-1, keepdims=True)
        centered = values - average
        spread = jnp.mean(centered * centered, axis=-1, keepdims=True)
        inverse = lax.rsqrt(spread + EPSILON)
        return centered * inverse, inverse

    def norm_one(load, index):
        base = index * T

        def body(rows, at):
            scaled, _ = moments(load(at))
            normed[rows, :] = (scaled * gain1 + shift1).astype(BF16)

        sub_rows(base, T, 64, body)

    def tok_own(at):
        return tok_own_ref[pl.ds(at, 64), :].astype(F32)

    def tok_other(at):
        return tok_in[pl.ds(at, 64), :].astype(F32)

    loads[0].wait()
    norm_one(tok_own, t)
    normed_copies = [send(normed.at[block_rows(t)], normed.at[block_rows(t)], (d, t_core))]
    tok_copy.wait_recv()
    fetch_fc.start()

    norm_one(tok_other, t_chip)
    normed_copies.append(
        send(normed.at[block_rows(t_chip)], normed.at[block_rows(t_chip)], (d, t_core))
    )
    for copy in info_copies:
        copy.wait_recv()

    half = info_buf[0, 2:3, 0:1]
    count = jnp.sum(info_buf[0, 1:2, :], axis=1, keepdims=True)
    for index in range(1, 4):
        count = count + jnp.sum(info_buf[index, 1:2, :], axis=1, keepdims=True)
    counts = [count * (1.0 - half), count * half]
    count_peers = [(d, t_chip)] + [(d_flip(bit), t) for bit in range(count_bits)]
    count_copies = []

    def count_start():
        step = len(count_copies)
        if step < len(count_peers):
            count_out[step, 0:1, :] = jnp.broadcast_to(counts[0], (1, 128))
            count_out[step, 1:2, :] = jnp.broadcast_to(counts[1], (1, 128))
            count_copies.append(send(count_out.at[step], count_in.at[step], count_peers[step]))

    def count_end():
        step = len(count_copies) - 1
        count_copies[step].wait_recv()
        counts[0] = counts[0] + count_in[step, 0:1, 0:1]
        counts[1] = counts[1] + count_in[step, 1:2, 0:1]

    count_start()
    seg_row = jnp.concatenate([info_buf[i, 0:1, :] for i in range(4)], axis=1)
    for index in range(4):
        row = jnp.broadcast_to(info_buf[index, 0:1, :], (128, T))
        seg_col[index * T : (index + 1) * T, :] = row.T
    for copy in normed_copies:
        copy.wait_recv()

    def project(side, weight):
        bias = (bias_own if side == 0 else bias_in)[1:2, 0:576]

        def body(rows, at):
            value = (dot(normed[rows, :], weight[...], NT) + bias).astype(BF16)
            for piece, ref in enumerate((q_s, k_s, v_s)):
                for h in range(3):
                    lane = piece * 192 + h * HD
                    ref[3 * side + h, rows, :] = value[:, lane : lane + HD]

        sub_rows(0, 4 * T, T, body)

    p_refs = (p0, p1, p2, p3)

    def attend(first):
        def head(h, carry):
            for index, p_ref in enumerate(p_refs):
                start, stop = index * T, (index + 1) * T
                rows = slice(start, stop)
                scores = dot(q_s[h, rows, :], k_s[h, 0:stop, :], NT) * EXP2_SCALE
                query_at = start + lax.broadcasted_iota(jnp.int32, (T, stop), 0)
                key_at = lax.broadcasted_iota(jnp.int32, (T, stop), 1)
                allowed = (key_at <= query_at) & (seg_col[rows, 0:1] == seg_row[:, 0:stop])
                scores = jnp.where(allowed, scores, -1e30)
                top = jnp.max(scores, axis=1, keepdims=True)
                exponent = jnp.exp2(scores - top)
                inverse = 1.0 / jnp.sum(exponent, axis=1, keepdims=True)
                low = (exponent * inverse).astype(BF16)
                p_ref[h] = low
                o_s[h, rows, :] = dot(low, v_s[h, 0:stop, :]).astype(BF16)
            return carry

        lax.fori_loop(first, first + 1, head, 0)

    loads[1].wait()
    fetch_qkv.share()
    fetch_proj.start()
    project(0, wqkv_ref)
    attend(0)
    fetch_out.share()
    cot_copy = send(cot_ref.at[1 - x], cot_in, (d, t_chip))
    attend(1)
    count_end()
    count_start()
    attend(2)
    fetch_qkv.cross()
    fetch_out.cross()
    fetch_fc.share()
    bias_copy.wait_recv()
    fetch_qkv.finish()
    project(1, wqkv_in)
    count_end()
    count_start()
    attend(3)
    fetch_proj.share()
    attend(4)
    attend(5)
    fetch_fc.cross()
    count_end()
    count_start()
    for h in range(6):
        att[:, h * HD : (h + 1) * HD] = o_s[h]

    def scatter(partial, give_ref, got_ref, before=()):
        for copy in before:
            links.wait_send(copy)
        copies = []
        for slot, index in enumerate((t_core, t_both)):
            give_ref[slot] = partial(index).astype(BF16)
            copies.append(send(give_ref.at[slot], got_ref.at[slot], (d, t_core)))
        for slot, index in enumerate((t, t_chip)):
            own[slot] = partial(index)
        return copies

    def out_partial(index):
        return dot(att[block_rows(index), :], wout_all[...])

    fetch_out.finish()
    loads[2].wait()
    attn_copies = scatter(out_partial, give, got)

    normed2_copies = []
    for slot, index in enumerate((t, t_chip)):
        attn_copies[slot].wait_recv()
        load = tok_own if slot == 0 else tok_other

        def body(rows, at, slot=slot, index=index, load=load):
            value = load(at) + own[slot, rows, :] + got[slot, rows, :].astype(F32) + out_bias
            middle[slot, rows, :] = value
            scaled, _ = moments(value)
            normed2[pl.ds(pl.multiple_of(index * T + at, 64), 64), :] = (
                scaled * gain2 + shift2
            ).astype(BF16)

        sub_rows(0, T, 64, body)
        rows = block_rows(index)
        normed2_copies.append(send(normed2.at[rows], normed2.at[rows], (d, t_core)))
    while len(count_copies) < len(count_peers):
        count_end()
        count_start()
    count_end()

    row_scale = (counts[0] + counts[1]) / (2.0 * jnp.where(half == 0.0, counts[0], counts[1]))
    cot_copy.wait_recv()
    for load in loads[3:]:
        load.wait()
    grad_copies = []
    for slot, index in enumerate((t, t_chip)):
        row = jnp.broadcast_to(info_buf[index, 1:2, :] * row_scale, (128, T))
        weight_col[slot] = row.T

    def out_grad(slot, rows, at):
        source = cot_own_ref[rows, :] if slot == 0 else cot_in[rows, :]
        return source.astype(F32) * weight_col[slot, rows, 0:1]

    for slot, index in enumerate((t, t_chip)):

        def body(rows, at, slot=slot, index=index):
            low = out_grad(slot, rows, at).astype(BF16)
            grad_full[pl.ds(pl.multiple_of(index * T + at, 64), 64), :] = low
            small_a[0, 5:6, :] += jnp.sum(low.astype(F32), axis=0, keepdims=True)

        sub_rows(0, T, 64, body)
        rows = block_rows(index)
        grad_copies.append(send(grad_full.at[rows], grad_full.at[rows], (d, t_core)))
    for copy in normed2_copies + grad_copies:
        copy.wait_recv()

    def mlp(side, fc, proj):
        bias = (bias_own if side == 0 else bias_in)[0:1, :]

        def body(rows, at):
            pre = dot(normed2[rows, :], fc[...]) + bias
            square = pre * pre
            bent = jnp.tanh(GELU_A * (pre + GELU_B * square * pre))
            rise = 0.5 * (1.0 + bent)
            hid[side, rows, :] = (pre * rise).astype(BF16)
            slope = rise + 0.5 * pre * (1.0 - bent * bent) * (
                GELU_A + (3.0 * GELU_A * GELU_B) * square
            )
            low = (dot(grad_full[rows, :], proj[...], NT) * slope).astype(BF16)
            dpre[side, rows, :] = low
            small_a[0, 6 + 2 * side : 7 + 2 * side, :] += jnp.sum(
                low.astype(F32), axis=0, keepdims=True
            )

        sub_rows(0, 4 * T, T, body)

    def proj_product(side, rows):
        return dot(hid[side, :, rows], grad_full[...], TN)

    def half_rows(index):
        return pl.ds(pl.multiple_of(index * 384, 384), 384)

    fetch_proj.cross()
    mlp(0, wfc_ref, wproj_ref)
    proj_give[0] = proj_product(0, half_rows(1 - y)).astype(BF16)
    proj_y = [send(proj_give.at[0], proj_got.at[0], (d_y, t))]
    fetch_fc.finish()
    fetch_proj.finish()
    mlp(1, wfc_in, wproj_in)
    proj_give[1] = proj_product(1, half_rows(1 - y)).astype(BF16)
    proj_y.append(send(proj_give.at[1], proj_got.at[1], (d_y, t)))

    def fc_product(side, chunk):
        return dot(normed2[:, chunk * 384 : (chunk + 1) * 384], dpre[side], TN)

    class Chunk:
        def __init__(self, slot, out, chunk, outer, acc_ref, low, raw, near_last=True):
            self.out, self.chunk, self.outer = out, chunk, outer
            self.near_last = near_last
            self.acc, self.low, self.raw = acc_ref, low, raw
            self.near_got, self.far_got = near_got.at[slot], far_got.at[slot]
            self.sem = local_sems.at[slot]
            self.half, self.fin = 96 * side_z, 96 * side_z + 48 * far_z

        def rows(self, start, size):
            return pl.ds(pl.multiple_of(start, 16), size)

        def total(self, rows):
            value = self.acc[rows, :]
            return value + self.low[rows, :].astype(F32) if self.raw else value

        def near_start(self):
            if self.raw:
                self.y_copy.wait_recv()
            rows = self.rows(96 - self.half, 96)
            self.low[rows, :] = self.total(rows).astype(BF16)
            self.near_copy = send(self.low.at[rows], self.near_got, (d_near, t))

        def far_start(self):
            self.near_copy.wait_recv()
            inner = self.rows(48 - 48 * far_z, 48)
            rows = self.rows(self.half + 48 - 48 * far_z, 48)
            value = self.total(rows) + self.near_got[inner, :].astype(F32)
            self.low[rows, :] = value.astype(BF16)
            self.far_copy = send(self.low.at[rows], self.far_got, (d_far, t))

        def placed(self, *rest):
            here = (self.chunk, y) if self.outer else (y, self.chunk)
            return self.out.at[here + rest]

        def far_back(self):
            inner = self.rows(48 * far_z, 48)
            rows = self.rows(self.fin, 48)
            value = self.total(rows) + self.near_got[inner, :].astype(F32)
            self.far_copy.wait_recv()
            value = value + self.far_got[...].astype(F32)
            self.low[rows, :] = value.astype(BF16)
            here, there = self.low.at[rows], self.placed(side_z, inner)
            self.keep = pltpu.make_async_copy(here, there, self.sem)
            self.keep.start()
            self.copy = send(here, there, (d_far, t))

        def back_one(self):
            self.keep.wait()
            self.copy.wait_recv()
            there = self.placed(side_z)
            self.copy = send(there, there, (d_y, t) if self.near_last else (d_near, t))

        def back_two(self):
            self.copy.wait_recv()
            if self.near_last:
                both = slice(None)
                here = (self.chunk, both) if self.outer else (both, self.chunk)
                there = self.out.at[here + (side_z,)]
                self.copy = send(there, there, (d_near, t))
            else:
                there = self.placed()
                self.copy = send(there, there, (d_y, t))

        def finish(self):
            self.copy.wait_recv()

    class Flow(Chunk):
        def __init__(self, slot, out, chunk, near_last):
            super().__init__(
                slot, out, chunk, True, acc.at[slot], y_got.at[slot], True, near_last
            )
            self.slot = slot
            self.x_copies = []

        def x_send(self, first=0, size=384):
            rows = slice(first, first + size)
            self.x_copies.append(
                send(x_give.at[self.slot, rows], x_got.at[self.slot, rows], (d, t_chip))
            )

        def y_start(self, fill):
            fill()
            for copy in self.x_copies:
                copy.wait_recv()
            slot = self.slot
            part[...] = part[...] + x_got[slot].astype(F32)
            other = pl.ds(pl.multiple_of((1 - y) * 192, 16), 192)
            mine = pl.ds(pl.multiple_of(y * 192, 16), 192)
            x_got[slot, other, :] = part[other, :].astype(BF16)
            self.y_copy = send(x_got.at[slot, other], y_got.at[slot], (d_y, t))
            acc[slot] = part[mine, :]

    fc_flows = [Flow(0, dfc_ref, 0, False), Flow(1, dfc_ref, 1, False)]
    attn_flows = [Flow(2, dattn_ref, 0, True), Flow(3, dattn_ref, 1, False)]
    proj_flows = []
    for chunk in range(2):
        rows = pl.ds(chunk * 192, 192)
        low = proj_got.at[0, rows]
        proj_flows.append(
            Chunk(4 + chunk, dproj_ref, chunk, False, proj_acc.at[rows], low, False)
        )

    def fc_fill(chunk):
        def fill():
            part[...] = fc_product(0, chunk)

        return fill

    for chunk in range(2):
        x_give[chunk] = fc_product(1, chunk).astype(BF16)
        fc_flows[chunk].x_send()

    def mlp_partial(index):
        rows = block_rows(index)
        return dot(hid[0, rows, :], wproj_ref[...]) + dot(hid[1, rows, :], wproj_in[...])

    mlp_copies = scatter(mlp_partial, give2, got2)
    for slot in range(2):
        mlp_copies[slot].wait_recv()

        def body(rows, at, slot=slot):
            value = (
                middle[slot, rows, :]
                + own[slot, rows, :]
                + got2[slot, rows, :].astype(F32)
                + proj_bias
            )
            (out_own, out_give)[slot][rows, :] = value.astype(BF16)

        sub_rows(0, T, 64, body)
    out_keep = pltpu.make_async_copy(out_own, out_ref.at[x], local_sems.at[7])
    out_keep.start()

    def norm2_partial(index):
        rows = block_rows(index)
        return dot(dpre[0, rows, :], wfc_ref[...], NT) + dot(dpre[1, rows, :], wfc_in[...], NT)

    back_copies = scatter(norm2_partial, give, got, attn_copies)
    def norm_back(upstream, values, gain):
        scaled, inverse = moments(values)
        pushed = upstream * gain
        mean_one = jnp.mean(pushed, axis=-1, keepdims=True)
        mean_two = jnp.mean(pushed * scaled, axis=-1, keepdims=True)
        gain_grad = jnp.sum(upstream * scaled, axis=0, keepdims=True)
        shift_grad = jnp.sum(upstream, axis=0, keepdims=True)
        return inverse * (pushed - mean_one - scaled * mean_two), gain_grad, shift_grad

    grad_copies = []
    for slot, index in enumerate((t, t_chip)):
        back_copies[slot].wait_recv()

        def body(rows, at, slot=slot, index=index):
            upstream = own[slot, rows, :] + got[slot, rows, :].astype(F32)
            part, gain_grad, shift_grad = norm_back(upstream, middle[slot, rows, :], gain2)
            value = out_grad(slot, rows, at) + part
            middle[slot, rows, :] = value
            low = value.astype(BF16)
            attn_grad[pl.ds(pl.multiple_of(index * T + at, 64), 64), :] = low
            small_a[0, 2:3, :] += gain_grad
            small_a[0, 3:4, :] += shift_grad
            small_a[0, 4:5, :] += jnp.sum(low.astype(F32), axis=0, keepdims=True)

        sub_rows(0, T, 64, body)
        rows = block_rows(index)
        grad_copies.append(send(attn_grad.at[rows], attn_grad.at[rows], (d, t_core)))
    for copy in grad_copies:
        copy.wait_recv()

    def spread_heads(rows, at):
        value = dot(attn_grad[rows, :], wout_all[...], NT)
        for h in range(6):
            do_s[h, rows, :] = value[:, h * HD : (h + 1) * HD].astype(BF16)

    sub_rows(0, 4 * T, T, spread_heads)
    x_give[3, 192:384, :] = dot(att[:, 192:384], attn_grad[...], TN).astype(BF16)

    def attend_back(first):
        def head(h, carry):
            query_t = q_s[h].T
            for index, p_ref in enumerate(p_refs):
                start, stop = index * T, (index + 1) * T
                rows = slice(start, stop)
                weights = p_ref[h]
                upstream = do_s[h, rows, :]
                row_dot = jnp.sum(
                    upstream.astype(F32) * o_s[h, rows, :].astype(F32), axis=1, keepdims=True
                )
                weight_grad = dot(upstream, v_s[h, 0:stop, :], NT)
                score_grad = (weights.astype(F32) * (weight_grad - row_dot)).astype(BF16)
                q_s[h, rows, :] = (dot(score_grad, k_s[h, 0:stop, :]) * SCALE).astype(BF16)
                key_part = dot(query_t[:, rows], score_grad)
                value_part = dot(upstream.T, weights)
                if start:
                    key_acc[:, 0:start] += key_part[:, 0:start]
                    value_acc[:, 0:start] += value_part[:, 0:start]
                key_acc[:, rows] = key_part[:, start:]
                value_acc[:, rows] = value_part[:, start:]
            k_s[h] = (key_acc[...] * SCALE).T.astype(BF16)
            v_s[h] = value_acc[...].T.astype(BF16)
            return carry

        lax.fori_loop(first, first + 1, head, 0)

    def dqkv_rows(side, first, last):
        return dqkv[side, :, first:last]

    def collect(side):
        for piece, ref in enumerate((q_s, k_s, v_s)):
            for h in range(3):
                lane = piece * 192 + h * HD
                dqkv[side, :, lane : lane + HD] = ref[3 * side + h]
        small_a[0, 7 + 2 * side : 8 + 2 * side, 0:576] = jnp.sum(
            dqkv[side, :, 0:576].astype(F32), axis=0, keepdims=True
        )

    attend_back(3)
    attend_back(4)
    attend_back(5)
    collect(1)
    x_give[3, 0:192, :] = dot(dqkv_rows(1, 384, 576), normed[...], TN).astype(BF16)
    attn_flows[1].x_send()
    x_give[2] = dot(dqkv_rows(1, 0, 384), normed[...], TN).astype(BF16)
    attn_flows[0].x_send()
    proj_y[1].wait_recv()
    mine = proj_product(1, half_rows(y)) + proj_got[1].astype(F32)
    proj_got[1] = mine.astype(BF16)
    proj_x = send(proj_got.at[1], proj_x_got, (d, t_chip))
    fc_flows[0].y_start(fc_fill(0))
    attend_back(0)
    fc_flows[1].y_start(fc_fill(1))
    proj_y[0].wait_recv()
    proj_acc[...] = proj_product(0, half_rows(y)) + proj_got[0].astype(F32)
    attend_back(1)
    fc_a, fc_b = fc_flows
    attn_a, attn_b = attn_flows
    proj_a, proj_b = proj_flows
    def attn_fill(chunk):
        def fill():
            if chunk == 0:
                part[...] = dot(dqkv_rows(0, 0, 384), normed[...], TN)
            else:
                part[0:192, :] = dot(dqkv_rows(0, 384, 576), normed[...], TN)
                part[192:384, :] = dot(att[:, 0:192], attn_grad[...], TN)

        return fill

    fc_a.near_start()
    attend_back(2)
    fc_a.far_start()
    collect(0)
    fc_b.near_start()

    def norm1_partial(index):
        rows = block_rows(index)
        return dot(dqkv[0, rows, 0:576], wqkv_ref[...]) + dot(dqkv[1, rows, 0:576], wqkv_in[...])

    back_copies = scatter(norm1_partial, give, got, back_copies)
    attn_b.y_start(attn_fill(1))
    fc_a.far_back()
    fc_b.far_start()
    for slot in (1, 0):
        back_copies[slot].wait_recv()
        load = tok_own if slot == 0 else tok_other

        def body(rows, at, slot=slot, load=load):
            upstream = own[slot, rows, :] + got[slot, rows, :].astype(F32)
            part, gain_grad, shift_grad = norm_back(upstream, load(at), gain1)
            value = middle[slot, rows, :] + part
            if slot == 0:
                own[0, rows, :] = value
            else:
                tg_give[rows, :] = value.astype(BF16)
            small_a[0, 0:1, :] += gain_grad
            small_a[0, 1:2, :] += shift_grad

        sub_rows(0, T, 64, body)
        if slot == 1:
            tg_copy = send(tg_give, tg_got, (d, t_chip))
    tg_keep = [pltpu.make_async_copy(own.at[0], tgrad_ref.at[x], local_sems.at[14])]
    tg_keep[0].start()

    small_peers = [(d_y, t), (d_near, t), (d_far, t), (d, t_core), (d, t_chip)]
    small_copies = []

    def small_next():
        step = len(small_copies)
        if step == 0:
            small_sum[0] = small_a[0]
        else:
            small_copies[-1].wait_recv()
            rows = 16 if step < 4 else 6
            small_sum[step] = small_sum[step - 1]
            small_sum[step, 0:rows, :] += small_in[step - 1, 0:rows, :]
        small_copies.append(send(small_sum.at[step], small_in.at[step], small_peers[step]))

    small_next()

    attn_b.near_start()
    fc_a.back_one()
    fc_b.far_back()
    attn_b.far_start()
    attn_a.y_start(attn_fill(0))
    fc_b.back_one()
    fc_a.back_two()
    small_next()
    attn_b.far_back()
    fc_b.back_two()
    attn_a.near_start()
    proj_x.wait_recv()
    proj_acc[...] += proj_x_got[...].astype(F32)
    proj_a.near_start()
    proj_b.near_start()
    attn_b.back_one()
    small_next()
    attn_a.far_start()
    out_copy = send(out_give, out_ref.at[x], (d, t_chip))
    proj_a.far_start()
    proj_b.far_start()
    attn_a.far_back()
    small_next()
    attn_b.back_two()
    proj_a.far_back()
    proj_b.far_back()
    attn_a.back_one()
    small_next()
    proj_a.back_one()
    proj_b.back_one()
    attn_a.back_two()
    proj_a.back_two()
    small_copies[4].wait_recv()
    small_ref[0:6, :] = small_sum[4, 0:6, :] + small_in[4, 0:6, :]
    small_ref[6:8, :] = small_sum[4, 6:8, :] + small_in[4, 8:10, :]
    proj_b.back_two()
    tg_copy.wait_recv()
    own[1] = tg_got[...].astype(F32)
    tg_keep.append(pltpu.make_async_copy(own.at[1], tgrad_ref.at[1 - x], local_sems.at[6]))
    tg_keep[1].start()
    out_copy.wait_recv()
    out_keep.wait()
    for flow in fc_flows + attn_flows + proj_flows:
        flow.finish()
    for copy in tg_keep:
        copy.wait()
    links.finish()


def finish_kernel(
    out_in, tgrad_in, dproj_in, dfc_in, dattn_in, small_in, out, tgrad, dproj, dfc, dqkv, dout, *small
):
    step = pl.program_id(0)
    out[...] = out_in[...]
    tgrad[...] = tgrad_in[...]
    dproj[...] = dproj_in[...].astype(F32)
    dfc[...] = dfc_in[...].astype(F32)

    @pl.when(step < 3)
    def _():
        dqkv[...] = dattn_in[...].astype(F32)

    @pl.when(step == 3)
    def _():
        dout[...] = dattn_in[...].astype(F32)
        for row, ref in enumerate(small[:7]):
            ref[...] = small_in[row, :]
        for piece in range(3):
            small[7][piece : piece + 1, :] = small_in[7:8, piece * 192 : (piece + 1) * 192]


def finish(output, tokens_grad, dproj, dfc, dattn, small):
    def rows(size, index):
        return pl.BlockSpec((size, 768), index)

    def same(i):
        return (i, 0)

    vector = jax.ShapeDtypeStruct((768,), F32)
    weight = jax.ShapeDtypeStruct((768, 768), F32)
    whole = pl.BlockSpec((768,), lambda i: (0,))
    return pl.pallas_call(
        finish_kernel,
        grid=(4,),
        out_shape=(
            jax.ShapeDtypeStruct((2 * T, 768), BF16),
            jax.ShapeDtypeStruct((2 * T, 768), F32),
            weight,
            weight,
            jax.ShapeDtypeStruct((576, 768), F32),
            jax.ShapeDtypeStruct((192, 768), F32),
        )
        + (vector,) * 7
        + (jax.ShapeDtypeStruct((3, 192), F32),),
        in_specs=[rows(128, same)] * 2
        + [rows(192, same)] * 3
        + [pl.BlockSpec((8, 768), lambda i: (0, 0))],
        out_specs=[rows(128, same)] * 2
        + [rows(192, same)] * 2
        + [rows(192, lambda i: (jnp.minimum(i, 2), 0)), rows(192, lambda i: (0, 0))]
        + [whole] * 7
        + [pl.BlockSpec((3, 192), lambda i: (0, 0))],
    )(output.reshape(2 * T, 768), tokens_grad.reshape(2 * T, 768), dproj, dfc, dattn, small)


VMEM = pl.BlockSpec(memory_space=pltpu.VMEM)
ANY = pl.BlockSpec(memory_space=pl.ANY)
SMEM = pl.BlockSpec(memory_space=pltpu.SMEM)


def local(
    dp_size,
    tokens,
    cotangent,
    segment_ids,
    valid_mask,
    row_half,
    norm1_gain,
    norm1_shift,
    qkv_weight,
    qkv_bias,
    out_weight,
    out_bias,
    norm2_gain,
    norm2_shift,
    fc_weight,
    fc_bias,
    proj_weight,
    proj_bias,
):
    qkv_rows = jnp.transpose(qkv_weight, (1, 2, 0)).reshape(576, 768)

    copies = 160

    def buffer(shape, dtype):
        return pltpu.VMEM(shape, dtype)

    outs = pl.pallas_call(
        functools.partial(layer_kernel, dp_size),
        out_shape=(
            jax.ShapeDtypeStruct((2, T, 768), BF16),
            jax.ShapeDtypeStruct((2, T, 768), F32),
            jax.ShapeDtypeStruct((2, 2, 2, 96, 768), BF16),
            jax.ShapeDtypeStruct((2, 2, 2, 96, 768), BF16),
            jax.ShapeDtypeStruct((2, 2, 2, 96, 768), BF16),
            jax.ShapeDtypeStruct((8, 768), F32),
        ),
        in_specs=[ANY] * 2 + [VMEM] * 2 + [SMEM] + [VMEM] * 8 + [ANY] * 4,
        out_specs=(ANY, ANY, ANY, ANY, ANY, VMEM),
        scratch_shapes=[
            buffer((T, 768), BF16),
            buffer((T, 768), BF16),
            buffer((576, 768), BF16),
            buffer((768, 768), BF16),
            buffer((768, 768), BF16),
            buffer((T, 768), BF16),
            buffer((T, 768), BF16),
            buffer((2, 8, T), F32),
            buffer((4, 8, T), F32),
            buffer((8, 768), F32),
            buffer((8, 768), F32),
            buffer((576, 768), BF16),
            buffer((384, 768), BF16),
            buffer((768, 768), BF16),
            buffer((768, 768), BF16),
            buffer((8, 8, 128), F32),
            buffer((8, 8, 128), F32),
            buffer((1024, 128), F32),
            buffer((2, T, 128), F32),
            buffer((1024, 768), BF16),
            buffer((1024, 768), BF16),
            buffer((1024, 768), BF16),
            buffer((1024, 768), BF16),
            buffer((6, 1024, HD), BF16),
            buffer((6, 1024, HD), BF16),
            buffer((6, 1024, HD), BF16),
            buffer((6, 1024, HD), BF16),
            buffer((6, 1024, HD), BF16),
            buffer((6, T, T), BF16),
            buffer((6, T, 2 * T), BF16),
            buffer((6, T, 3 * T), BF16),
            buffer((6, T, 4 * T), BF16),
            buffer((1024, 384), BF16),
            buffer((2, T, 768), F32),
            buffer((2, 1024, 768), BF16),
            buffer((2, 1024, 768), BF16),
            buffer((2, T, 768), BF16),
            buffer((2, T, 768), BF16),
            buffer((2, T, 768), F32),
            buffer((2, T, 768), BF16),
            buffer((2, T, 768), BF16),
            buffer((HD, 1024), F32),
            buffer((HD, 1024), F32),
            buffer((384, 768), F32),
            buffer((2, 384, 768), BF16),
            buffer((2, 384, 768), BF16),
            buffer((384, 768), BF16),
            buffer((6, 96, 768), BF16),
            buffer((6, 48, 768), BF16),
            buffer((384, 768), F32),
            buffer((4, 192, 768), F32),
            buffer((4, 384, 768), BF16),
            buffer((4, 384, 768), BF16),
            buffer((4, 192, 768), BF16),
            buffer((T, 768), BF16),
            buffer((T, 768), BF16),
            buffer((T, 768), BF16),
            buffer((T, 768), BF16),
            buffer((1, 16, 768), F32),
            buffer((5, 16, 768), F32),
            buffer((5, 16, 768), F32),
            pltpu.SemaphoreType.DMA((copies,)),
            pltpu.SemaphoreType.DMA((copies,)),
            pltpu.SemaphoreType.DMA((15,)),
        ],
        compiler_params=pltpu.CompilerParams(
            collective_id=0, has_side_effects=True, vmem_limit_bytes=66500000
        ),
    )(
        tokens,
        cotangent,
        segment_ids,
        valid_mask,
        row_half,
        norm1_gain,
        norm1_shift,
        qkv_bias,
        out_bias,
        norm2_gain,
        norm2_shift,
        fc_bias,
        proj_bias,
        qkv_rows,
        out_weight,
        fc_weight,
        proj_weight,
    )
    output, tokens_grad, dproj, dfc, dattn, small = outs

    def all_groups(value):
        if dp_size == GROUP:
            return value
        sets = [[g * GROUP + i for g in range(dp_size // GROUP)] for i in range(GROUP)]
        return lax.psum(value.astype(F32), "dp", axis_index_groups=sets)

    dproj, dfc, dattn = (value.reshape(768, 768) for value in (dproj, dfc, dattn))
    dproj, dfc, dattn, small = map(all_groups, (dproj, dfc, dattn, small))
    outs = finish(output, tokens_grad, dproj, dfc, dattn, small)
    output, tokens_grad, dproj, dfc, dqkv, dout = outs[:6]
    gain1, shift1, gain2, shift2, dout_bias, dproj_bias, dfc_bias, dqkv_bias = outs[6:]
    return (
        output.reshape(2, T, 768),
        tokens_grad.reshape(2, T, 768),
        gain1,
        shift1,
        jnp.transpose(dqkv.reshape(3, 192, 768), (2, 0, 1)),
        dqkv_bias,
        dout,
        dout_bias,
        gain2,
        shift2,
        dfc,
        dfc_bias,
        dproj,
        dproj_bias,
    )


def solution(mesh):
    row, flat = P("dp", "tp", None), P("dp", "tp")
    in_specs = (
        row,
        row,
        flat,
        flat,
        P("dp"),
        P(),
        P(),
        P(None, None, "tp"),
        P(None, "tp"),
        P("tp", None),
        P(),
        P(),
        P(),
        P(None, "tp"),
        P("tp"),
        P("tp", None),
        P(),
    )
    out_specs = (
        row,
        row,
        P(),
        P(),
        P(None, None, "tp"),
        P(None, "tp"),
        P("tp", None),
        P(),
        P(),
        P(),
        P(None, "tp"),
        P("tp"),
        P("tp", None),
        P(),
    )
    return jax.shard_map(
        functools.partial(local, mesh.shape["dp"]),
        mesh=mesh,
        in_specs=in_specs,
        out_specs=out_specs,
        check_vma=False,
    )
```

```python
import functools

import jax
import jax.numpy as jnp
from jax import lax
from jax.experimental import pallas as pl
from jax.experimental.pallas import tpu as pltpu
from jax.sharding import PartitionSpec as P

HD = 64
EPSILON = 1e-05
SCALE = HD ** (-0.5)
EXP2_SCALE = SCALE * 1.4426950408889634
GELU_A = 0.7978845608028654
GELU_B = 0.044715
T = 256
F32 = jnp.float32
BF16 = jnp.bfloat16
NN = (((1,), (0,)), ((), ()))
NT = (((1,), (1,)), ((), ()))
TN = (((0,), (0,)), ((), ()))
MESH = pl.DeviceIdType.MESH
GROUP = 8


def dot(a, b, dims=NN):
    return lax.dot_general(a, b, dims, preferred_element_type=F32)


def sub_rows(base, size, chunk, body):
    def step(i, carry):
        body(pl.ds(pl.multiple_of(base + i * chunk, chunk), chunk), i * chunk)
        return carry

    lax.fori_loop(0, size // chunk, step, 0)


class Links:
    def __init__(self, send_sems, recv_sems):
        self.send_sems, self.recv_sems = send_sems, recv_sems
        self.copies = []
        self.sent = []

    def send(self, source, target, device):
        index = len(self.copies)
        copy = pltpu.make_async_remote_copy(
            src_ref=source,
            dst_ref=target,
            send_sem=self.send_sems.at[index],
            recv_sem=self.recv_sems.at[index],
            device_id=device,
            device_id_type=MESH,
        )
        copy.start()
        self.copies.append(copy)
        return copy

    def wait_send(self, copy):
        copy.wait_send()
        self.sent.append(copy)

    def finish(self):
        for copy in self.copies:
            if not any(copy is other for other in self.sent):
                copy.wait_send()


def layer_kernel(
    dp_size,
    tok_ref,
    cot_ref,
    seg_ref,
    valid_ref,
    half_ref,
    gain1_ref,
    shift1_ref,
    qkv_bias_ref,
    out_bias_ref,
    gain2_ref,
    shift2_ref,
    fc_bias_ref,
    proj_bias_ref,
    wqkv_hbm,
    wout_hbm,
    wfc_hbm,
    wproj_hbm,
    out_ref,
    tgrad_ref,
    dproj_ref,
    dfc_ref,
    dattn_ref,
    small_ref,
    tok_own_ref,
    cot_own_ref,
    wqkv_ref,
    wfc_ref,
    wproj_ref,
    tok_in,
    cot_in,
    info_own,
    info_buf,
    bias_own,
    bias_in,
    wqkv_in,
    wout_all,
    wfc_in,
    wproj_in,
    count_out,
    count_in,
    seg_col,
    weight_col,
    normed,
    normed2,
    grad_full,
    attn_grad,
    q_s,
    k_s,
    v_s,
    o_s,
    do_s,
    p0,
    p1,
    p2,
    p3,
    att,
    middle,
    hid,
    dpre,
    give,
    got,
    own,
    give2,
    got2,
    key_acc,
    value_acc,
    proj_acc,
    proj_give,
    proj_got,
    proj_x_got,
    near_got,
    far_got,
    part,
    acc,
    x_give,
    x_got,
    y_got,
    out_own,
    out_give,
    tg_give,
    tg_got,
    small_a,
    small_sum,
    small_in,
    send_sems,
    recv_sems,
    local_sems,
):
    d = lax.axis_index("dp")
    t = lax.axis_index("tp")
    x = t // 2
    c = t - 2 * x
    t_core = t + 1 - 2 * c
    t_chip = lax.rem(t + 2, 4)
    t_both = 3 - t
    y = lax.rem(d, 2)
    group_first = d - lax.rem(d, GROUP)
    place = d - group_first
    z = place // 2
    d_y = d + 1 - 2 * y
    side_z = lax.rem(z, 2)
    far_z = z // 2
    d_near = d + 2 - 4 * side_z
    d_far = d + 4 - 8 * far_z
    fourth = 2 * y + side_z

    def d_flip(bit):
        size = 1 << bit
        return d + size - 2 * size * lax.rem(d // size, 2)

    dqkv = dpre
    count_bits = dp_size.bit_length() - 1
    links = Links(send_sems, recv_sems)
    send = links.send

    barrier = pltpu.get_barrier_semaphore()
    peers = [(d, t_core), (d, t_chip), (d, t_both)]
    peers += [(group_first + lax.rem(place + k, GROUP), t) for k in range(1, GROUP)]
    peers += [(d_flip(bit), t) for bit in range(3, count_bits)]
    for peer in peers:
        pl.semaphore_signal(barrier, inc=1, device_id=peer, device_id_type=MESH)
    loads = [
        pltpu.make_async_copy(source, target, local_sems.at[8 + index])
        for index, (source, target) in enumerate(
            (
                (tok_ref.at[x], tok_own_ref),
                (wqkv_hbm, wqkv_ref),
                (wout_hbm, wout_all.at[0:192]),
                (cot_ref.at[x], cot_own_ref),
                (wfc_hbm, wfc_ref),
                (wproj_hbm, wproj_ref),
            )
        )
    ]
    for load in loads:
        load.start()

    def block_rows(index):
        return pl.ds(pl.multiple_of(index * T, T), T)

    gain1, shift1, out_bias, gain2, shift2, proj_bias = (
        ref[...].reshape(1, 768)
        for ref in (gain1_ref, shift1_ref, out_bias_ref, gain2_ref, shift2_ref, proj_bias_ref)
    )

    for row in range(2):
        info_own[row, 0:1, :] = seg_ref[row : row + 1, :].astype(F32)
        info_own[row, 1:2, :] = valid_ref[row : row + 1, :].astype(F32)
        info_own[row, 2:3, :] = jnp.full((1, T), half_ref[row], jnp.int32).astype(F32)
        info_own[row, 3:8, :] = jnp.zeros((5, T), F32)
    bias_own[...] = jnp.zeros_like(bias_own)
    bias_own[0:1, :] = fc_bias_ref[...].reshape(1, 768)
    for piece in range(3):
        bias_own[1:2, piece * 192 : (piece + 1) * 192] = qkv_bias_ref[piece : piece + 1, :]
    info_buf[t] = info_own[x]
    for ref in (small_a, count_out):
        ref[...] = jnp.zeros_like(ref)

    pl.semaphore_wait(barrier, len(peers))
    info_copies = [
        send(info_own.at[x], info_buf.at[t], (d, t_core)),
        send(info_own.at[1 - x], info_buf.at[t], (d, t_chip)),
        send(info_own.at[1 - x], info_buf.at[t], (d, t_both)),
    ]
    bias_copy = send(bias_own, bias_in, (d, t_chip))
    tok_copy = send(tok_ref.at[1 - x], tok_in, (d, t_chip))

    class Fetch:
        def __init__(self, source, target, base, rows, first):
            self.source, self.target, self.base = source, target, base
            self.quarter, self.first, self.state = rows // 4, first, 0

        def view(self, ref, base, index, start, size):
            offset = pl.multiple_of(base + index * self.quarter + start, 16)
            return ref.at[pl.ds(offset, size)]

        def mine(self, index, start=0, size=None):
            return self.view(self.target, self.base, index, start, size or self.quarter)

        def start(self):
            here = self.view(self.source, 0, fourth, 0, self.quarter)
            self.copy = send(here, self.mine(fourth), (d, t_chip))

        def share(self):
            self.copy.wait_recv()
            here = self.mine(fourth)
            self.y_copy = send(here, here, (d_y, t))
            self.z_copy = send(here, here, (d_near, t))

        def cross(self):
            from_y = fourth + 2 - 4 * y
            from_z = fourth + 1 - 2 * side_z
            self.y_copy.wait_recv()
            here = self.mine(from_y, 0, self.first)
            self.last = [send(here, here, (d_near, t))]
            self.z_copy.wait_recv()
            here = self.mine(from_z, self.first, self.quarter - self.first)
            self.last.append(send(here, here, (d_y, t)))

        def finish(self):
            for copy in self.last:
                copy.wait_recv()

    fetch_qkv = Fetch(wqkv_hbm, wqkv_in, 0, 576, 80)
    fetch_out = Fetch(wout_hbm, wout_all, 192, 192, 32)
    fetch_fc = Fetch(wfc_hbm, wfc_in, 0, 768, 96)
    fetch_proj = Fetch(wproj_hbm, wproj_in, 0, 768, 96)
    fetch_qkv.start()
    fetch_out.start()

    def moments(values):
        average = jnp.mean(values, axis=-1, keepdims=True)
        centered = values - average
        spread = jnp.mean(centered * centered, axis=-1, keepdims=True)
        inverse = lax.rsqrt(spread + EPSILON)
        return centered * inverse, inverse

    def norm_one(load, index):
        base = index * T

        def body(rows, at):
            scaled, _ = moments(load(at))
            normed[rows, :] = (scaled * gain1 + shift1).astype(BF16)

        sub_rows(base, T, 64, body)

    def tok_own(at):
        return tok_own_ref[pl.ds(at, 64), :].astype(F32)

    def tok_other(at):
        return tok_in[pl.ds(at, 64), :].astype(F32)

    loads[0].wait()
    norm_one(tok_own, t)
    normed_copies = [send(normed.at[block_rows(t)], normed.at[block_rows(t)], (d, t_core))]
    tok_copy.wait_recv()
    fetch_fc.start()

    norm_one(tok_other, t_chip)
    normed_copies.append(
        send(normed.at[block_rows(t_chip)], normed.at[block_rows(t_chip)], (d, t_core))
    )
    for copy in info_copies:
        copy.wait_recv()

    half = info_buf[0, 2:3, 0:1]
    count = jnp.sum(info_buf[0, 1:2, :], axis=1, keepdims=True)
    for index in range(1, 4):
        count = count + jnp.sum(info_buf[index, 1:2, :], axis=1, keepdims=True)
    counts = [count * (1.0 - half), count * half]
    count_peers = [(d, t_chip)] + [(d_flip(bit), t) for bit in range(count_bits)]
    count_copies = []

    def count_start():
        step = len(count_copies)
        if step < len(count_peers):
            count_out[step, 0:1, :] = jnp.broadcast_to(counts[0], (1, 128))
            count_out[step, 1:2, :] = jnp.broadcast_to(counts[1], (1, 128))
            count_copies.append(send(count_out.at[step], count_in.at[step], count_peers[step]))

    def count_end():
        step = len(count_copies) - 1
        count_copies[step].wait_recv()
        counts[0] = counts[0] + count_in[step, 0:1, 0:1]
        counts[1] = counts[1] + count_in[step, 1:2, 0:1]

    count_start()
    seg_row = jnp.concatenate([info_buf[i, 0:1, :] for i in range(4)], axis=1)
    for index in range(4):
        row = jnp.broadcast_to(info_buf[index, 0:1, :], (128, T))
        seg_col[index * T : (index + 1) * T, :] = row.T
    for copy in normed_copies:
        copy.wait_recv()

    def project(side, weight):
        bias = (bias_own if side == 0 else bias_in)[1:2, 0:576]

        def body(rows, at):
            value = (dot(normed[rows, :], weight[...], NT) + bias).astype(BF16)
            for piece, ref in enumerate((q_s, k_s, v_s)):
                for h in range(3):
                    lane = piece * 192 + h * HD
                    ref[3 * side + h, rows, :] = value[:, lane : lane + HD]

        sub_rows(0, 4 * T, T, body)

    p_refs = (p0, p1, p2, p3)

    def attend(first):
        def head(h, carry):
            for index, p_ref in enumerate(p_refs):
                start, stop = index * T, (index + 1) * T
                rows = slice(start, stop)
                scores = dot(q_s[h, rows, :], k_s[h, 0:stop, :], NT) * EXP2_SCALE
                query_at = start + lax.broadcasted_iota(jnp.int32, (T, stop), 0)
                key_at = lax.broadcasted_iota(jnp.int32, (T, stop), 1)
                allowed = (key_at <= query_at) & (seg_col[rows, 0:1] == seg_row[:, 0:stop])
                scores = jnp.where(allowed, scores, -1e30)
                top = jnp.max(scores, axis=1, keepdims=True)
                exponent = jnp.exp2(scores - top)
                inverse = 1.0 / jnp.sum(exponent, axis=1, keepdims=True)
                low = (exponent * inverse).astype(BF16)
                p_ref[h] = low
                o_s[h, rows, :] = dot(low, v_s[h, 0:stop, :]).astype(BF16)
            return carry

        lax.fori_loop(first, first + 1, head, 0)

    loads[1].wait()
    fetch_qkv.share()
    fetch_proj.start()
    project(0, wqkv_ref)
    attend(0)
    fetch_out.share()
    cot_copy = send(cot_ref.at[1 - x], cot_in, (d, t_chip))
    attend(1)
    count_end()
    count_start()
    attend(2)
    fetch_qkv.cross()
    fetch_out.cross()
    fetch_fc.share()
    bias_copy.wait_recv()
    fetch_qkv.finish()
    project(1, wqkv_in)
    count_end()
    count_start()
    attend(3)
    fetch_proj.share()
    attend(4)
    attend(5)
    fetch_fc.cross()
    count_end()
    count_start()
    for h in range(6):
        att[:, h * HD : (h + 1) * HD] = o_s[h]

    def scatter(partial, give_ref, got_ref, before=()):
        for copy in before:
            links.wait_send(copy)
        copies = []
        for slot, index in enumerate((t_core, t_both)):
            give_ref[slot] = partial(index).astype(BF16)
            copies.append(send(give_ref.at[slot], got_ref.at[slot], (d, t_core)))
        for slot, index in enumerate((t, t_chip)):
            own[slot] = partial(index)
        return copies

    def out_partial(index):
        return dot(att[block_rows(index), :], wout_all[...])

    fetch_out.finish()
    loads[2].wait()
    attn_copies = scatter(out_partial, give, got)

    normed2_copies = []
    for slot, index in enumerate((t, t_chip)):
        attn_copies[slot].wait_recv()
        load = tok_own if slot == 0 else tok_other

        def body(rows, at, slot=slot, index=index, load=load):
            value = load(at) + own[slot, rows, :] + got[slot, rows, :].astype(F32) + out_bias
            middle[slot, rows, :] = value
            scaled, _ = moments(value)
            normed2[pl.ds(pl.multiple_of(index * T + at, 64), 64), :] = (
                scaled * gain2 + shift2
            ).astype(BF16)

        sub_rows(0, T, 64, body)
        rows = block_rows(index)
        normed2_copies.append(send(normed2.at[rows], normed2.at[rows], (d, t_core)))
    while len(count_copies) < len(count_peers):
        count_end()
        count_start()
    count_end()

    row_scale = (counts[0] + counts[1]) / (2.0 * jnp.where(half == 0.0, counts[0], counts[1]))
    cot_copy.wait_recv()
    for load in loads[3:]:
        load.wait()
    grad_copies = []
    for slot, index in enumerate((t, t_chip)):
        row = jnp.broadcast_to(info_buf[index, 1:2, :] * row_scale, (128, T))
        weight_col[slot] = row.T

    def out_grad(slot, rows, at):
        source = cot_own_ref[rows, :] if slot == 0 else cot_in[rows, :]
        return source.astype(F32) * weight_col[slot, rows, 0:1]

    for slot, index in enumerate((t, t_chip)):

        def body(rows, at, slot=slot, index=index):
            low = out_grad(slot, rows, at).astype(BF16)
            grad_full[pl.ds(pl.multiple_of(index * T + at, 64), 64), :] = low
            small_a[0, 5:6, :] += jnp.sum(low.astype(F32), axis=0, keepdims=True)

        sub_rows(0, T, 64, body)
        rows = block_rows(index)
        grad_copies.append(send(grad_full.at[rows], grad_full.at[rows], (d, t_core)))
    for copy in normed2_copies + grad_copies:
        copy.wait_recv()

    def mlp(side, fc, proj):
        bias = (bias_own if side == 0 else bias_in)[0:1, :]

        def body(rows, at):
            pre = dot(normed2[rows, :], fc[...]) + bias
            square = pre * pre
            bent = jnp.tanh(GELU_A * (pre + GELU_B * square * pre))
            rise = 0.5 * (1.0 + bent)
            hid[side, rows, :] = (pre * rise).astype(BF16)
            slope = rise + 0.5 * pre * (1.0 - bent * bent) * (
                GELU_A + (3.0 * GELU_A * GELU_B) * square
            )
            low = (dot(grad_full[rows, :], proj[...], NT) * slope).astype(BF16)
            dpre[side, rows, :] = low
            small_a[0, 6 + 2 * side : 7 + 2 * side, :] += jnp.sum(
                low.astype(F32), axis=0, keepdims=True
            )

        sub_rows(0, 4 * T, T, body)

    def proj_product(side, rows):
        return dot(hid[side, :, rows], grad_full[...], TN)

    def half_rows(index):
        return pl.ds(pl.multiple_of(index * 384, 384), 384)

    fetch_proj.cross()
    mlp(0, wfc_ref, wproj_ref)
    proj_give[0] = proj_product(0, half_rows(1 - y)).astype(BF16)
    proj_y = [send(proj_give.at[0], proj_got.at[0], (d_y, t))]
    fetch_fc.finish()
    fetch_proj.finish()
    mlp(1, wfc_in, wproj_in)
    proj_give[1] = proj_product(1, half_rows(1 - y)).astype(BF16)
    proj_y.append(send(proj_give.at[1], proj_got.at[1], (d_y, t)))

    def fc_product(side, chunk):
        return dot(normed2[:, chunk * 384 : (chunk + 1) * 384], dpre[side], TN)

    class Chunk:
        def __init__(self, slot, out, chunk, outer, acc_ref, low, raw, near_last=True):
            self.out, self.chunk, self.outer = out, chunk, outer
            self.near_last = near_last
            self.acc, self.low, self.raw = acc_ref, low, raw
            self.near_got, self.far_got = near_got.at[slot], far_got.at[slot]
            self.sem = local_sems.at[slot]
            self.half, self.fin = 96 * side_z, 96 * side_z + 48 * far_z

        def rows(self, start, size):
            return pl.ds(pl.multiple_of(start, 16), size)

        def total(self, rows):
            value = self.acc[rows, :]
            return value + self.low[rows, :].astype(F32) if self.raw else value

        def near_start(self):
            if self.raw:
                self.y_copy.wait_recv()
            rows = self.rows(96 - self.half, 96)
            self.low[rows, :] = self.total(rows).astype(BF16)
            self.near_copy = send(self.low.at[rows], self.near_got, (d_near, t))

        def far_start(self):
            self.near_copy.wait_recv()
            inner = self.rows(48 - 48 * far_z, 48)
            rows = self.rows(self.half + 48 - 48 * far_z, 48)
            value = self.total(rows) + self.near_got[inner, :].astype(F32)
            self.low[rows, :] = value.astype(BF16)
            self.far_copy = send(self.low.at[rows], self.far_got, (d_far, t))

        def placed(self, *rest):
            here = (self.chunk, y) if self.outer else (y, self.chunk)
            return self.out.at[here + rest]

        def far_back(self):
            inner = self.rows(48 * far_z, 48)
            rows = self.rows(self.fin, 48)
            value = self.total(rows) + self.near_got[inner, :].astype(F32)
            self.far_copy.wait_recv()
            value = value + self.far_got[...].astype(F32)
            self.low[rows, :] = value.astype(BF16)
            here, there = self.low.at[rows], self.placed(side_z, inner)
            self.keep = pltpu.make_async_copy(here, there, self.sem)
            self.keep.start()
            self.copy = send(here, there, (d_far, t))

        def back_one(self):
            self.keep.wait()
            self.copy.wait_recv()
            there = self.placed(side_z)
            self.copy = send(there, there, (d_y, t) if self.near_last else (d_near, t))

        def back_two(self):
            self.copy.wait_recv()
            if self.near_last:
                both = slice(None)
                here = (self.chunk, both) if self.outer else (both, self.chunk)
                there = self.out.at[here + (side_z,)]
                self.copy = send(there, there, (d_near, t))
            else:
                there = self.placed()
                self.copy = send(there, there, (d_y, t))

        def finish(self):
            self.copy.wait_recv()

    class Flow(Chunk):
        def __init__(self, slot, out, chunk, near_last):
            super().__init__(
                slot, out, chunk, True, acc.at[slot], y_got.at[slot], True, near_last
            )
            self.slot = slot
            self.x_copies = []

        def x_send(self, first=0, size=384):
            rows = slice(first, first + size)
            self.x_copies.append(
                send(x_give.at[self.slot, rows], x_got.at[self.slot, rows], (d, t_chip))
            )

        def y_start(self, fill):
            fill()
            for copy in self.x_copies:
                copy.wait_recv()
            slot = self.slot
            part[...] = part[...] + x_got[slot].astype(F32)
            other = pl.ds(pl.multiple_of((1 - y) * 192, 16), 192)
            mine = pl.ds(pl.multiple_of(y * 192, 16), 192)
            x_got[slot, other, :] = part[other, :].astype(BF16)
            self.y_copy = send(x_got.at[slot, other], y_got.at[slot], (d_y, t))
            acc[slot] = part[mine, :]

    fc_flows = [Flow(0, dfc_ref, 0, False), Flow(1, dfc_ref, 1, False)]
    attn_flows = [Flow(2, dattn_ref, 0, True), Flow(3, dattn_ref, 1, False)]
    proj_flows = []
    for chunk in range(2):
        rows = pl.ds(chunk * 192, 192)
        low = proj_got.at[0, rows]
        proj_flows.append(
            Chunk(4 + chunk, dproj_ref, chunk, False, proj_acc.at[rows], low, False)
        )

    def fc_fill(chunk):
        def fill():
            part[...] = fc_product(0, chunk)

        return fill

    for chunk in range(2):
        x_give[chunk] = fc_product(1, chunk).astype(BF16)
        fc_flows[chunk].x_send()

    def mlp_partial(index):
        rows = block_rows(index)
        return dot(hid[0, rows, :], wproj_ref[...]) + dot(hid[1, rows, :], wproj_in[...])

    def norm2_partial(index):
        rows = block_rows(index)
        return dot(dpre[0, rows, :], wfc_ref[...], NT) + dot(dpre[1, rows, :], wfc_in[...], NT)

    back_copies = scatter(norm2_partial, give, got, attn_copies)
    def norm_back(upstream, values, gain):
        scaled, inverse = moments(values)
        pushed = upstream * gain
        mean_one = jnp.mean(pushed, axis=-1, keepdims=True)
        mean_two = jnp.mean(pushed * scaled, axis=-1, keepdims=True)
        gain_grad = jnp.sum(upstream * scaled, axis=0, keepdims=True)
        shift_grad = jnp.sum(upstream, axis=0, keepdims=True)
        return inverse * (pushed - mean_one - scaled * mean_two), gain_grad, shift_grad

    grad_copies = []
    for slot, index in enumerate((t, t_chip)):
        back_copies[slot].wait_recv()

        def body(rows, at, slot=slot, index=index):
            upstream = own[slot, rows, :] + got[slot, rows, :].astype(F32)
            part, gain_grad, shift_grad = norm_back(upstream, middle[slot, rows, :], gain2)
            value = out_grad(slot, rows, at) + part
            (out_own, out_give)[slot][rows, :] = (middle[slot, rows, :] + proj_bias).astype(BF16)
            middle[slot, rows, :] = value
            low = value.astype(BF16)
            attn_grad[pl.ds(pl.multiple_of(index * T + at, 64), 64), :] = low
            small_a[0, 2:3, :] += gain_grad
            small_a[0, 3:4, :] += shift_grad
            small_a[0, 4:5, :] += jnp.sum(low.astype(F32), axis=0, keepdims=True)

        sub_rows(0, T, 64, body)
        rows = block_rows(index)
        grad_copies.append(send(attn_grad.at[rows], attn_grad.at[rows], (d, t_core)))
    for copy in grad_copies:
        copy.wait_recv()

    def spread_heads(rows, at):
        value = dot(attn_grad[rows, :], wout_all[...], NT)
        for h in range(6):
            do_s[h, rows, :] = value[:, h * HD : (h + 1) * HD].astype(BF16)

    sub_rows(0, 4 * T, T, spread_heads)
    x_give[3, 192:384, :] = dot(att[:, 192:384], attn_grad[...], TN).astype(BF16)

    def attend_back(first):
        def head(h, carry):
            query_t = q_s[h].T
            for index, p_ref in enumerate(p_refs):
                start, stop = index * T, (index + 1) * T
                rows = slice(start, stop)
                weights = p_ref[h]
                upstream = do_s[h, rows, :]
                row_dot = jnp.sum(
                    upstream.astype(F32) * o_s[h, rows, :].astype(F32), axis=1, keepdims=True
                )
                weight_grad = dot(upstream, v_s[h, 0:stop, :], NT)
                score_grad = (weights.astype(F32) * (weight_grad - row_dot)).astype(BF16)
                q_s[h, rows, :] = (dot(score_grad, k_s[h, 0:stop, :]) * SCALE).astype(BF16)
                key_part = dot(query_t[:, rows], score_grad)
                value_part = dot(upstream.T, weights)
                if start:
                    key_acc[:, 0:start] += key_part[:, 0:start]
                    value_acc[:, 0:start] += value_part[:, 0:start]
                key_acc[:, rows] = key_part[:, start:]
                value_acc[:, rows] = value_part[:, start:]
            k_s[h] = (key_acc[...] * SCALE).T.astype(BF16)
            v_s[h] = value_acc[...].T.astype(BF16)
            return carry

        lax.fori_loop(first, first + 1, head, 0)

    def dqkv_rows(side, first, last):
        return dqkv[side, :, first:last]

    def collect(side):
        for piece, ref in enumerate((q_s, k_s, v_s)):
            for h in range(3):
                lane = piece * 192 + h * HD
                dqkv[side, :, lane : lane + HD] = ref[3 * side + h]
        small_a[0, 7 + 2 * side : 8 + 2 * side, 0:576] = jnp.sum(
            dqkv[side, :, 0:576].astype(F32), axis=0, keepdims=True
        )

    attend_back(3)
    attend_back(4)
    attend_back(5)
    collect(1)
    x_give[3, 0:192, :] = dot(dqkv_rows(1, 384, 576), normed[...], TN).astype(BF16)
    attn_flows[1].x_send()
    x_give[2] = dot(dqkv_rows(1, 0, 384), normed[...], TN).astype(BF16)
    attn_flows[0].x_send()
    proj_y[1].wait_recv()
    mine = proj_product(1, half_rows(y)) + proj_got[1].astype(F32)
    proj_got[1] = mine.astype(BF16)
    proj_x = send(proj_got.at[1], proj_x_got, (d, t_chip))
    fc_flows[0].y_start(fc_fill(0))
    mlp_copies = scatter(mlp_partial, give2, got2)
    for slot in range(2):
        mlp_copies[slot].wait_recv()

        def body(rows, at, slot=slot):
            value = (
                (out_own, out_give)[slot][rows, :].astype(F32)
                + own[slot, rows, :]
                + got2[slot, rows, :].astype(F32)
            )
            (out_own, out_give)[slot][rows, :] = value.astype(BF16)

        sub_rows(0, T, 64, body)
    out_keep = pltpu.make_async_copy(out_own, out_ref.at[x], local_sems.at[7])
    out_keep.start()
    attend_back(0)
    fc_flows[1].y_start(fc_fill(1))
    proj_y[0].wait_recv()
    proj_acc[...] = proj_product(0, half_rows(y)) + proj_got[0].astype(F32)
    attend_back(1)
    fc_a, fc_b = fc_flows
    attn_a, attn_b = attn_flows
    proj_a, proj_b = proj_flows
    def attn_fill(chunk):
        def fill():
            if chunk == 0:
                part[...] = dot(dqkv_rows(0, 0, 384), normed[...], TN)
            else:
                part[0:192, :] = dot(dqkv_rows(0, 384, 576), normed[...], TN)
                part[192:384, :] = dot(att[:, 0:192], attn_grad[...], TN)

        return fill

    fc_a.near_start()
    attend_back(2)
    fc_a.far_start()
    collect(0)
    fc_b.near_start()

    def norm1_partial(index):
        rows = block_rows(index)
        return dot(dqkv[0, rows, 0:576], wqkv_ref[...]) + dot(dqkv[1, rows, 0:576], wqkv_in[...])

    back_copies = scatter(norm1_partial, give, got, back_copies)
    attn_b.y_start(attn_fill(1))
    fc_a.far_back()
    fc_b.far_start()
    for slot in (1, 0):
        back_copies[slot].wait_recv()
        load = tok_own if slot == 0 else tok_other

        def body(rows, at, slot=slot, load=load):
            upstream = own[slot, rows, :] + got[slot, rows, :].astype(F32)
            part, gain_grad, shift_grad = norm_back(upstream, load(at), gain1)
            value = middle[slot, rows, :] + part
            if slot == 0:
                own[0, rows, :] = value
            else:
                tg_give[rows, :] = value.astype(BF16)
            small_a[0, 0:1, :] += gain_grad
            small_a[0, 1:2, :] += shift_grad

        sub_rows(0, T, 64, body)
        if slot == 1:
            tg_copy = send(tg_give, tg_got, (d, t_chip))
    tg_keep = [pltpu.make_async_copy(own.at[0], tgrad_ref.at[x], local_sems.at[14])]
    tg_keep[0].start()

    small_peers = [(d_y, t), (d_near, t), (d_far, t), (d, t_core), (d, t_chip)]
    small_copies = []

    def small_next():
        step = len(small_copies)
        if step == 0:
            small_sum[0] = small_a[0]
        else:
            small_copies[-1].wait_recv()
            rows = 16 if step < 4 else 6
            small_sum[step] = small_sum[step - 1]
            small_sum[step, 0:rows, :] += small_in[step - 1, 0:rows, :]
        small_copies.append(send(small_sum.at[step], small_in.at[step], small_peers[step]))

    small_next()

    attn_b.near_start()
    fc_a.back_one()
    fc_b.far_back()
    attn_b.far_start()
    attn_a.y_start(attn_fill(0))
    fc_b.back_one()
    fc_a.back_two()
    small_next()
    attn_b.far_back()
    fc_b.back_two()
    attn_a.near_start()
    proj_x.wait_recv()
    proj_acc[...] += proj_x_got[...].astype(F32)
    proj_a.near_start()
    proj_b.near_start()
    attn_b.back_one()
    small_next()
    attn_a.far_start()
    out_copy = send(out_give, out_ref.at[x], (d, t_chip))
    proj_a.far_start()
    proj_b.far_start()
    attn_a.far_back()
    small_next()
    attn_b.back_two()
    proj_a.far_back()
    proj_b.far_back()
    attn_a.back_one()
    small_next()
    proj_a.back_one()
    proj_b.back_one()
    attn_a.back_two()
    proj_a.back_two()
    small_copies[4].wait_recv()
    small_ref[0:6, :] = small_sum[4, 0:6, :] + small_in[4, 0:6, :]
    small_ref[6:8, :] = small_sum[4, 6:8, :] + small_in[4, 8:10, :]
    proj_b.back_two()
    tg_copy.wait_recv()
    own[1] = tg_got[...].astype(F32)
    tg_keep.append(pltpu.make_async_copy(own.at[1], tgrad_ref.at[1 - x], local_sems.at[6]))
    tg_keep[1].start()
    out_copy.wait_recv()
    out_keep.wait()
    for flow in fc_flows + attn_flows + proj_flows:
        flow.finish()
    for copy in tg_keep:
        copy.wait()
    links.finish()


def finish_kernel(
    out_in, tgrad_in, dproj_in, dfc_in, dattn_in, small_in, out, tgrad, dproj, dfc, dqkv, dout, *small
):
    step = pl.program_id(0)
    out[...] = out_in[...]
    tgrad[...] = tgrad_in[...]
    dproj[...] = dproj_in[...].astype(F32)
    dfc[...] = dfc_in[...].astype(F32)

    @pl.when(step < 3)
    def _():
        dqkv[...] = dattn_in[...].astype(F32)

    @pl.when(step == 3)
    def _():
        dout[...] = dattn_in[...].astype(F32)
        for row, ref in enumerate(small[:7]):
            ref[...] = small_in[row, :]
        for piece in range(3):
            small[7][piece : piece + 1, :] = small_in[7:8, piece * 192 : (piece + 1) * 192]


def finish(output, tokens_grad, dproj, dfc, dattn, small):
    def rows(size, index):
        return pl.BlockSpec((size, 768), index)

    def same(i):
        return (i, 0)

    vector = jax.ShapeDtypeStruct((768,), F32)
    weight = jax.ShapeDtypeStruct((768, 768), F32)
    whole = pl.BlockSpec((768,), lambda i: (0,))
    return pl.pallas_call(
        finish_kernel,
        grid=(4,),
        out_shape=(
            jax.ShapeDtypeStruct((2 * T, 768), BF16),
            jax.ShapeDtypeStruct((2 * T, 768), F32),
            weight,
            weight,
            jax.ShapeDtypeStruct((576, 768), F32),
            jax.ShapeDtypeStruct((192, 768), F32),
        )
        + (vector,) * 7
        + (jax.ShapeDtypeStruct((3, 192), F32),),
        in_specs=[rows(128, same)] * 2
        + [rows(192, same)] * 3
        + [pl.BlockSpec((8, 768), lambda i: (0, 0))],
        out_specs=[rows(128, same)] * 2
        + [rows(192, same)] * 2
        + [rows(192, lambda i: (jnp.minimum(i, 2), 0)), rows(192, lambda i: (0, 0))]
        + [whole] * 7
        + [pl.BlockSpec((3, 192), lambda i: (0, 0))],
    )(output.reshape(2 * T, 768), tokens_grad.reshape(2 * T, 768), dproj, dfc, dattn, small)


VMEM = pl.BlockSpec(memory_space=pltpu.VMEM)
ANY = pl.BlockSpec(memory_space=pl.ANY)
SMEM = pl.BlockSpec(memory_space=pltpu.SMEM)


def local(
    dp_size,
    tokens,
    cotangent,
    segment_ids,
    valid_mask,
    row_half,
    norm1_gain,
    norm1_shift,
    qkv_weight,
    qkv_bias,
    out_weight,
    out_bias,
    norm2_gain,
    norm2_shift,
    fc_weight,
    fc_bias,
    proj_weight,
    proj_bias,
):
    qkv_rows = jnp.transpose(qkv_weight, (1, 2, 0)).reshape(576, 768)

    copies = 160

    def buffer(shape, dtype):
        return pltpu.VMEM(shape, dtype)

    outs = pl.pallas_call(
        functools.partial(layer_kernel, dp_size),
        out_shape=(
            jax.ShapeDtypeStruct((2, T, 768), BF16),
            jax.ShapeDtypeStruct((2, T, 768), F32),
            jax.ShapeDtypeStruct((2, 2, 2, 96, 768), BF16),
            jax.ShapeDtypeStruct((2, 2, 2, 96, 768), BF16),
            jax.ShapeDtypeStruct((2, 2, 2, 96, 768), BF16),
            jax.ShapeDtypeStruct((8, 768), F32),
        ),
        in_specs=[ANY] * 2 + [VMEM] * 2 + [SMEM] + [VMEM] * 8 + [ANY] * 4,
        out_specs=(ANY, ANY, ANY, ANY, ANY, VMEM),
        scratch_shapes=[
            buffer((T, 768), BF16),
            buffer((T, 768), BF16),
            buffer((576, 768), BF16),
            buffer((768, 768), BF16),
            buffer((768, 768), BF16),
            buffer((T, 768), BF16),
            buffer((T, 768), BF16),
            buffer((2, 8, T), F32),
            buffer((4, 8, T), F32),
            buffer((8, 768), F32),
            buffer((8, 768), F32),
            buffer((576, 768), BF16),
            buffer((384, 768), BF16),
            buffer((768, 768), BF16),
            buffer((768, 768), BF16),
            buffer((8, 8, 128), F32),
            buffer((8, 8, 128), F32),
            buffer((1024, 128), F32),
            buffer((2, T, 128), F32),
            buffer((1024, 768), BF16),
            buffer((1024, 768), BF16),
            buffer((1024, 768), BF16),
            buffer((1024, 768), BF16),
            buffer((6, 1024, HD), BF16),
            buffer((6, 1024, HD), BF16),
            buffer((6, 1024, HD), BF16),
            buffer((6, 1024, HD), BF16),
            buffer((6, 1024, HD), BF16),
            buffer((6, T, T), BF16),
            buffer((6, T, 2 * T), BF16),
            buffer((6, T, 3 * T), BF16),
            buffer((6, T, 4 * T), BF16),
            buffer((1024, 384), BF16),
            buffer((2, T, 768), F32),
            buffer((2, 1024, 768), BF16),
            buffer((2, 1024, 768), BF16),
            buffer((2, T, 768), BF16),
            buffer((2, T, 768), BF16),
            buffer((2, T, 768), F32),
            buffer((2, T, 768), BF16),
            buffer((2, T, 768), BF16),
            buffer((HD, 1024), F32),
            buffer((HD, 1024), F32),
            buffer((384, 768), F32),
            buffer((2, 384, 768), BF16),
            buffer((2, 384, 768), BF16),
            buffer((384, 768), BF16),
            buffer((6, 96, 768), BF16),
            buffer((6, 48, 768), BF16),
            buffer((384, 768), F32),
            buffer((4, 192, 768), F32),
            buffer((4, 384, 768), BF16),
            buffer((4, 384, 768), BF16),
            buffer((4, 192, 768), BF16),
            buffer((T, 768), BF16),
            buffer((T, 768), BF16),
            buffer((T, 768), BF16),
            buffer((T, 768), BF16),
            buffer((1, 16, 768), F32),
            buffer((5, 16, 768), F32),
            buffer((5, 16, 768), F32),
            pltpu.SemaphoreType.DMA((copies,)),
            pltpu.SemaphoreType.DMA((copies,)),
            pltpu.SemaphoreType.DMA((15,)),
        ],
        compiler_params=pltpu.CompilerParams(
            collective_id=0, has_side_effects=True, vmem_limit_bytes=66500000
        ),
    )(
        tokens,
        cotangent,
        segment_ids,
        valid_mask,
        row_half,
        norm1_gain,
        norm1_shift,
        qkv_bias,
        out_bias,
        norm2_gain,
        norm2_shift,
        fc_bias,
        proj_bias,
        qkv_rows,
        out_weight,
        fc_weight,
        proj_weight,
    )
    output, tokens_grad, dproj, dfc, dattn, small = outs

    def all_groups(value):
        if dp_size == GROUP:
            return value
        sets = [[g * GROUP + i for g in range(dp_size // GROUP)] for i in range(GROUP)]
        return lax.psum(value.astype(F32), "dp", axis_index_groups=sets)

    dproj, dfc, dattn = (value.reshape(768, 768) for value in (dproj, dfc, dattn))
    dproj, dfc, dattn, small = map(all_groups, (dproj, dfc, dattn, small))
    outs = finish(output, tokens_grad, dproj, dfc, dattn, small)
    output, tokens_grad, dproj, dfc, dqkv, dout = outs[:6]
    gain1, shift1, gain2, shift2, dout_bias, dproj_bias, dfc_bias, dqkv_bias = outs[6:]
    return (
        output.reshape(2, T, 768),
        tokens_grad.reshape(2, T, 768),
        gain1,
        shift1,
        jnp.transpose(dqkv.reshape(3, 192, 768), (2, 0, 1)),
        dqkv_bias,
        dout,
        dout_bias,
        gain2,
        shift2,
        dfc,
        dfc_bias,
        dproj,
        dproj_bias,
    )


def solution(mesh):
    row, flat = P("dp", "tp", None), P("dp", "tp")
    in_specs = (
        row,
        row,
        flat,
        flat,
        P("dp"),
        P(),
        P(),
        P(None, None, "tp"),
        P(None, "tp"),
        P("tp", None),
        P(),
        P(),
        P(),
        P(None, "tp"),
        P("tp"),
        P("tp", None),
        P(),
    )
    out_specs = (
        row,
        row,
        P(),
        P(),
        P(None, None, "tp"),
        P(None, "tp"),
        P("tp", None),
        P(),
        P(),
        P(),
        P(None, "tp"),
        P("tp"),
        P("tp", None),
        P(),
    )
    return jax.shard_map(
        functools.partial(local, mesh.shape["dp"]),
        mesh=mesh,
        in_specs=in_specs,
        out_specs=out_specs,
        check_vma=False,
    )
```
